128 devices in a mesh: dp: 16 (over y_lo, x, core), feat: 8 (over z, y_hi).
Axes of the slice: x: 4, y: 4 (y_hi: 2, y_lo: 2; y = y_hi * 2 + y_lo), z: 4, core: 2. Of those that a mesh axis runs over, the one named last changes fastest.
Arguments:
- activations: bfloat16 [16384, 8192], P('dp', 'feat'), may hold values from -6 to 6
- gradients: bfloat16 [16384, 8192], P('dp', 'feat'), may hold values from -6 to 6
- start_act: float32 [8192, 128], P('feat'), may hold values from -6 to 6
- start_grad: float32 [8192, 128], P('feat'), may hold values from -6 to 6
- doc_ids: int32 [16384], P('dp'), may hold values from 0 to 31, never falling along the last dimension, each value on 1 to 1024 neighbouring positions
Outputs:
- basis_act: float32 [8192, 128], P('feat')
- basis_grad: float32 [8192, 128], P('feat')
- scales: float32 [128, 128], replicated
The draws below stay inside these ranges and needn't reach their ends.
Inputs may be any that keep to these rules, and one draw needn't show every extreme that they name: `doc_ids`: each document's tokens are consecutive and in order of id; every id occurs, and some document has exactly 1024 tokens.
All inputs are finite; a program needn't handle non-finite values.
Results may differ from the reference program's by a relative error of at most 0.0003.
Values sent between devices are 32-bit elements; how exact they have to be, the bound alone decides.
A program may use at most 64 MiB of HBM per device.

```python
import math
import jax
import jax.numpy as jnp
import numpy as np
from jax import lax

D = 8192
K = 128
ITERS = 6
TOKENS = 16384
DOCS = 32
MAXDOC = 1024


def block_scale(key, extent, pieces, smallest, high):
    def one(dim, blocks):
        heights = jax.random.uniform(jax.random.fold_in(jax.random.fold_in(key, 6), dim), (blocks,), jnp.float32, smallest / len(pieces), high / len(pieces))
        return jnp.repeat(jnp.exp(heights), extent[dim] // blocks).reshape((-1,) + (1,) * (len(extent) - dim - 1))

    gain = one(*pieces[0])
    for cut in pieces[1:]:
        gain = gain * one(*cut)
    return gain


def length_profile(amount, total, bound, skew):
    weights = [(1 << 20) // math.isqrt(grade ** skew) + 1 for grade in range(2, amount + 1)]
    surplus, given = total - bound - (amount - 1), [1] * (amount - 1)
    while surplus > 0:
        candidates = [i for i in range(amount - 1) if given[i] < bound]
        whole, remaining = sum([weights[i] for i in candidates]), surplus
        for i in candidates:
            addition = min(bound - given[i], max(1, remaining * weights[i] // whole), surplus)
            given[i] = given[i] + addition
            surplus = surplus - addition
    return np.array([bound] + given)


def ragged(rng, number_of, total, most, slope):
    if number_of == 2:
        one = jax.random.randint(rng, (), max(1, total - most), min(most, total - 1) + 1)
        return jnp.stack([one, total - one])
    tallies = jnp.asarray(length_profile(number_of, total, most, slope), jnp.int32)
    pairs = (number_of - 1) // 2
    giver, sink = tallies[1:1 + 2 * pairs:2], tallies[2:2 + 2 * pairs:2]
    margin = jnp.minimum(giver - 1, most - sink)
    passed = jax.random.randint(jax.random.fold_in(rng, 1), (pairs,), 0, 1 << 20) % (margin + 1)
    tallies = tallies.at[1:1 + 2 * pairs:2].set(giver - passed).at[2:2 + 2 * pairs:2].set(sink + passed)
    return tallies[jax.random.permutation(jax.random.fold_in(rng, 2), number_of)]


def scatter_about(key, dims, scale, most, shards=(), kind=jnp.bfloat16):
    loudness = block_scale(key, dims, shards, -0.22, 0.18) if shards else 1.0
    result = jax.random.normal(key, dims, jnp.float32) * scale * loudness
    return jnp.minimum(jnp.maximum(result, -most), most).astype(kind)


def setup_inputs(seed: int = 0) -> dict:
    key_of = jax.random.split(jax.random.key(seed), 6)
    return {
        "activations": scatter_about(key_of[0], (TOKENS, D), 1.0, 6.0, ((0, 16), (1, 8))),
        "gradients": scatter_about(key_of[1], (TOKENS, D), 1.0, 6.0, ((0, 16), (1, 8))),
        "start_act": scatter_about(key_of[2], (D, K), 1.0, 6.0, ((0, 8),), jnp.float32),
        "start_grad": scatter_about(key_of[3], (D, K), 1.0, 6.0, ((0, 8),), jnp.float32),
        "doc_ids": jnp.searchsorted(jnp.cumsum(ragged(key_of[4], DOCS, TOKENS, MAXDOC, 2)), jnp.arange(TOKENS), side="right").astype(jnp.int32),
    }


highest = lax.Precision.HIGHEST

def gram_of(image):
    return lax.dot_general(image, image, (((0,), (0,)), ((), ())), precision=highest)

def orthonormal(image, gram_mat):
    lower = jnp.linalg.cholesky(gram_mat)
    return jax.scipy.linalg.solve_triangular(lower, image.T, lower=True).T

def covariance_times(wide, basis):
    projected = jnp.dot(wide, basis, precision=highest)
    return lax.dot_general(wide, projected, (((0,), (0,)), ((), ())), precision=highest)

def reference(activations, gradients, start_act, start_grad, doc_ids):
    act_wide = activations.astype(jnp.float32)
    grad_wide = gradients.astype(jnp.float32)
    basis_act = start_act
    basis_grad = start_grad
    for sweep in range(ITERS):
        image_act = covariance_times(act_wide, basis_act)
        image_grad = covariance_times(grad_wide, basis_grad)
        basis_act = orthonormal(image_act, gram_of(image_act))
        basis_grad = orthonormal(image_grad, gram_of(image_grad))
    proj_act = jnp.dot(act_wide, basis_act, precision=highest)
    proj_grad = jnp.dot(grad_wide, basis_grad, precision=highest)
    onehot = (doc_ids[:, None] == jnp.arange(DOCS, dtype=jnp.int32)[None, :]).astype(jnp.float32)
    counts = jnp.sum(onehot, axis=0)
    weight = jnp.dot(onehot, 1.0 / (DOCS * counts), precision=highest)
    left = weight[:, None] * proj_grad * proj_grad
    scales = lax.dot_general(left, proj_act * proj_act, (((0,), (0,)), ((), ())), precision=highest)
    return (basis_act, basis_grad, scales)
```

```python
import functools

import jax
import jax.numpy as jnp
from jax import lax
from jax.experimental import pallas as pl
from jax.experimental.pallas import tpu as pltpu
from jax.sharding import PartitionSpec as P

ITERS = 6
K = 128
MESH = pl.DeviceIdType.MESH
F32 = jnp.float32
BF16 = jnp.bfloat16
HIGHEST = lax.Precision.HIGHEST

OFFSETS = ((2, 1), (1, 1), (3, 1), (2, 0), (0, 1), (1, 0), (3, 0))


def pieces(value):
    high = value.astype(BF16)
    rest = value - high.astype(F32)
    mid = rest.astype(BF16)
    low = (rest - mid.astype(F32)).astype(BF16)
    return jnp.concatenate([high, mid, low], axis=1)


def joined(product):
    return product[:, :K] + (product[:, K : 2 * K] + product[:, 2 * K :])


def times(a, b):
    return lax.dot_general(a, b, (((1,), (0,)), ((), ())), preferred_element_type=F32)


def full(a, b, contract):
    return lax.dot_general(
        a, b, ((contract[:1], contract[1:]), ((), ())), precision=HIGHEST, preferred_element_type=F32
    )


def kernel(
    act_ref, grad_ref, start_act_ref, start_grad_ref, ids_ref,
    basis_act_ref, basis_grad_ref, scales_ref,
    x_send, x_recv, x, xt, split,
    y_send, y_recv, p, v_send, v_recv, v,
    g_send, g_recv, g, work, inverse,
    ids, c_recv, proj_mine, proj_other, basis_mine, basis_other,
    s_part, s_feat, s_dp, s_mine, s_other,
    x_sems, y_ssem, y_rsem, p_ssem, p_rsem, v_ssem, v_rsem, w_ssem, w_rsem,
    gs_ssem, gs_rsem, ga_ssem, ga_rsem, c_ssem, c_rsem, core_ssem, core_rsem,
    sf_ssem, sf_rsem, sd_ssem, sd_rsem,
):
    dp, feat = lax.axis_index("dp"), lax.axis_index("feat")
    core, q = dp % 2, dp // 2
    px, py = q % 4, q // 4
    fz, fy = feat // 2, feat % 2

    def feat_peer(r):
        dz, dy = OFFSETS[r]
        return ((fz + dz) % 4) * 2 + (fy + dy) % 2

    def feat_from(r):
        dz, dy = OFFSETS[r]
        return ((fz + 4 - dz) % 4) * 2 + (fy + dy) % 2

    def q_peer(r):
        dx, dy = OFFSETS[r]
        return ((py + dy) % 2) * 4 + (px + dx) % 4

    def q_from(r):
        dx, dy = OFFSETS[r]
        return ((py + dy) % 2) * 4 + (px + 4 - dx) % 4

    def to_feat(r, src, dst, ssem, rsem):
        return pltpu.make_async_remote_copy(
            src_ref=src, dst_ref=dst, send_sem=ssem.at[r], recv_sem=rsem.at[r],
            device_id={"feat": feat_peer(r)}, device_id_type=MESH,
        )

    def to_dp(r, src, dst, ssem, rsem):
        return pltpu.make_async_remote_copy(
            src_ref=src, dst_ref=dst, send_sem=ssem.at[r], recv_sem=rsem.at[r],
            device_id={"dp": q_peer(r) * 2 + core}, device_id_type=MESH,
        )

    def to_core(i, src, dst):
        return pltpu.make_async_remote_copy(
            src_ref=src, dst_ref=dst, send_sem=core_ssem.at[i], recv_sem=core_rsem.at[i],
            device_id={"dp": q * 2 + (1 - core)}, device_id_type=MESH,
        )

    barrier = pltpu.get_barrier_semaphore()
    for r in range(7):
        pl.semaphore_signal(barrier, inc=1, device_id={"feat": feat_peer(r)}, device_id_type=MESH)
        pl.semaphore_signal(
            barrier, inc=1, device_id={"dp": q_peer(r) * 2 + core}, device_id_type=MESH
        )
    pl.semaphore_signal(
        barrier, inc=1, device_id={"dp": q * 2 + (1 - core)}, device_id_type=MESH
    )
    pl.semaphore_wait(barrier, 15)

    even = core == 0
    ids_own = pl.ds(pl.multiple_of(core * 8, 8), 8)
    ids[ids_own, :] = ids_ref[...]
    ids_copy = to_core(0, ids.at[ids_own, :], ids.at[ids_own, :])
    ids_copy.start()
    x_copies = []
    for i in range(4):
        rows = slice(i * 256, (i + 1) * 256)
        x_send[rows, :] = jnp.where(even, grad_ref[rows, :].astype(F32), act_ref[rows, :].astype(F32))
        copy = pltpu.make_async_remote_copy(
            src_ref=x_send.at[rows, :], dst_ref=x_recv.at[rows, :],
            send_sem=x_sems.at[0, i], recv_sem=x_sems.at[1, i],
            device_id={"dp": q * 2 + (1 - core)}, device_id_type=MESH,
        )
        copy.start()
        x_copies.append(copy)
    for i in range(4):
        rows = slice(i * 256, (i + 1) * 256)
        x[pl.ds(pl.multiple_of(core * 1024 + i * 256, 256), 256), :] = jnp.where(
            even, act_ref[rows, :].astype(F32), grad_ref[rows, :].astype(F32)
        ).astype(BF16)
    v[...] = jnp.where(even, start_act_ref[...], start_grad_ref[...])
    lane = lax.broadcasted_iota(jnp.int32, (K, K), 1)
    row = lax.broadcasted_iota(jnp.int32, (K, K), 0)
    inverse[...] = (lane == row).astype(F32)
    for i in range(4):
        x_copies[i].wait()
        x[pl.ds(pl.multiple_of((1 - core) * 1024 + i * 256, 256), 256), :] = x_recv[
            i * 256 : (i + 1) * 256, :
        ].astype(BF16)

    def token_rows(f):
        return pl.ds(pl.multiple_of(f * 256, 256), 256)

    def feature_rows(i):
        return pl.ds(pl.multiple_of(i * 128, 128), 128)

    def gram_rows(f):
        return pl.ds(pl.multiple_of(f * 16, 16), 16)

    def project():
        split[...] = pieces(v[...])
        copies = []
        for r in range(7):
            rows = token_rows(feat_peer(r))
            y_send[rows, :] = joined(times(x[rows, :], split[...]))
            copy = to_feat(r, y_send.at[rows, :], y_recv.at[r], y_ssem, y_rsem)
            copy.start()
            copies.append(copy)
        rows = token_rows(feat)
        y_send[rows, :] = joined(times(x[rows, :], split[...]))
        return copies

    def projected(copies):
        for copy in copies:
            copy.wait()
        total = y_send[token_rows(feat), :]
        for r in range(7):
            total = total + y_recv[r]
        return total

    def gram_send():
        image = v[...]
        g_send[...] = full(image, image, (0, 0))
        copies = []
        for r in range(7):
            copy = to_feat(r, g_send.at[gram_rows(feat_peer(r)), :], g_recv.at[r], gs_ssem, gs_rsem)
            copy.start()
            copies.append(copy)
        return copies

    def gram_copies():
        return [
            to_feat(r, g_send.at[gram_rows(feat_peer(r)), :], g_recv.at[r], gs_ssem, gs_rsem)
            for r in range(7)
        ]

    def gram_gathers():
        mine = gram_rows(feat)
        return [to_feat(r, g.at[mine, :], g.at[mine, :], ga_ssem, ga_rsem) for r in range(7)]

    def gram_sum():
        for copy in gram_copies():
            copy.wait()
        total = g_send[gram_rows(feat), :]
        for r in range(7):
            total = total + g_recv[r]
        g[gram_rows(feat), :] = total
        for copy in gram_gathers():
            copy.start()

    def factor():
        for copy in gram_gathers():
            copy.wait()
        work[:, :K] = g[...]
        work[:, K:] = (lane == row).astype(F32)
        small_row = lax.broadcasted_iota(jnp.int32, (8, K), 0)
        small_lane = lax.broadcasted_iota(jnp.int32, (8, K), 1)
        wide_row = lax.broadcasted_iota(jnp.int32, (K, 2 * K), 0)

        def panel(i, _):
            at = pl.ds(pl.multiple_of(i * 8, 8), 8)
            strip = work[at, :]
            block = pltpu.roll(strip[:, :K], (K - i * 8) % K, 1)
            block = jnp.where(small_lane < 8, block, (small_lane - 8 == small_row).astype(F32))
            for j in range(8):
                column = block[:, j : j + 1]
                pivot = block[j : j + 1, j : j + 1]
                scale = lax.rsqrt(pivot)
                scale = scale * (1.5 - 0.5 * pivot * scale * scale)
                normal = block[j : j + 1, :] * scale
                below = block - (column * scale) * normal
                block = jnp.where(small_row > j, below, jnp.where(small_row == j, normal, block))
            fresh = jnp.zeros_like(strip)
            for j in range(8):
                fresh = fresh + block[:, 8 + j : 9 + j] * strip[j : j + 1, :]
            update = full(fresh[:, :K], fresh, (0, 0))
            work[...] = jnp.where(wide_row >= i * 8 + 8, work[...] - update, work[...])
            work[at, :] = fresh
            return 0

        lax.fori_loop(0, 16, panel, 0)
        inverse[...] = work[:, K:]

    def sweep(step, _):
        y_copies = project()

        @pl.when(step > 0)
        def _():
            gram_send()

        @pl.when(step == 0)
        def _():
            for c in range(8):
                xt[c] = x[c * 256 : (c + 1) * 256, :].T

        total = projected(y_copies)
        mine = token_rows(feat)
        p[mine, :] = total
        p_copies = [to_feat(r, p.at[mine, :], p.at[mine, :], p_ssem, p_rsem) for r in range(7)]

        @pl.when(step > 0)
        def _():
            gram_sum()

        for copy in p_copies:
            copy.start()
        v_send[...] = joined(times(xt[feat], pieces(p[mine, :])))

        @pl.when(step > 0)
        def _():
            factor()

        for r in reversed(range(7)):
            p_copies[r].wait()
            source = feat_from(r)
            v_send[...] += joined(times(xt[source], pieces(p[token_rows(source), :])))

        own = feature_rows(q)
        v_copies = []
        for r in range(7):
            copy = to_dp(r, v_send.at[feature_rows(q_peer(r)), :], v_recv.at[r], v_ssem, v_rsem)
            copy.start()
            v_copies.append(copy)
        for copy in v_copies:
            copy.wait()
        total = v_send[own, :]
        for r in range(7):
            total = total + v_recv[r]
        v[own, :] = full(total, inverse[...], (1, 1))
        w_copies = [to_dp(r, v.at[own, :], v.at[own, :], w_ssem, w_rsem) for r in range(7)]
        for copy in w_copies:
            copy.start()
        for copy in w_copies:
            copy.wait()
        return 0

    lax.fori_loop(0, ITERS, sweep, 0)

    y_copies = project()
    gram_send()
    ids_copy.wait()
    counts = jnp.zeros((1, K), F32)
    for i in range(16):
        column = jnp.broadcast_to(ids[i : i + 1, :].astype(F32), (K, K)).T
        counts = counts + jnp.sum((column == lane.astype(F32)).astype(F32), axis=0, keepdims=True)
    c_recv[q] = jnp.broadcast_to(counts, (8, K))
    c_copies = [to_dp(r, c_recv.at[q], c_recv.at[q], c_ssem, c_rsem) for r in range(7)]
    for copy in c_copies:
        copy.start()

    total = projected(y_copies)
    gram_sum()
    factor()
    basis_mine[...] = full(v[...], inverse[...], (1, 1))
    proj_mine[...] = full(total, inverse[...], (1, 1))
    proj_copy = to_core(1, proj_mine, proj_other)
    proj_copy.start()
    basis_copy = to_core(2, basis_mine, basis_other)
    basis_copy.start()
    for copy in c_copies:
        copy.wait()
    counts = c_recv[0]
    for i in range(1, 8):
        counts = counts + c_recv[i]
    counts = counts[0:1, :]
    documents = 2 * lax.axis_size("dp")
    share = jnp.where(counts > 0, 1.0 / (documents * jnp.maximum(counts, 1.0)), 0.0)
    weight = []
    for i in range(2):
        column = jnp.broadcast_to(ids[pl.ds(feat * 2 + i, 1), :].astype(F32), (K, K)).T
        weight.append(
            jnp.sum(jnp.where(column == lane.astype(F32), share, 0.0), axis=1, keepdims=True)
        )
    proj_copy.wait()
    proj_act = jnp.where(even, proj_mine[...], proj_other[...])
    proj_grad = jnp.where(even, proj_other[...], proj_mine[...])
    left = jnp.concatenate(weight, axis=0) * proj_grad * proj_grad
    s_part[...] = full(left, proj_act * proj_act, (0, 0))

    half = pl.ds(pl.multiple_of(core * 64, 64), 64)
    s_feat[feat] = s_part[half, :]
    copies = [to_feat(r, s_feat.at[feat], s_feat.at[feat], sf_ssem, sf_rsem) for r in range(7)]
    for copy in copies:
        copy.start()
    for copy in copies:
        copy.wait()
    total = s_feat[0]
    for i in range(1, 8):
        total = total + s_feat[i]
    s_dp[q] = total
    copies = [to_dp(r, s_dp.at[q], s_dp.at[q], sd_ssem, sd_rsem) for r in range(7)]
    for copy in copies:
        copy.start()
    basis_copy.wait()
    basis_act_ref[...] = jnp.where(even, basis_mine[...], basis_other[...])
    basis_grad_ref[...] = jnp.where(even, basis_other[...], basis_mine[...])
    for copy in copies:
        copy.wait()
    total = s_dp[0]
    for i in range(1, 8):
        total = total + s_dp[i]
    s_mine[...] = total
    s_copy = to_core(3, s_mine, s_other)
    s_copy.start()
    s_copy.wait()
    scales_ref[half, :] = s_mine[...]
    scales_ref[pl.ds(pl.multiple_of((1 - core) * 64, 64), 64), :] = s_other[...]


def local(activations, gradients, start_act, start_grad, doc_ids):
    vmem = pl.BlockSpec(memory_space=pltpu.VMEM)
    dma = pltpu.SemaphoreType.DMA
    return pl.pallas_call(
        kernel,
        out_shape=(
            jax.ShapeDtypeStruct((1024, K), F32),
            jax.ShapeDtypeStruct((1024, K), F32),
            jax.ShapeDtypeStruct((K, K), F32),
        ),
        in_specs=[vmem] * 5,
        out_specs=(vmem,) * 3,
        scratch_shapes=[
            pltpu.VMEM((1024, 1024), F32),
            pltpu.VMEM((1024, 1024), F32),
            pltpu.VMEM((2048, 1024), BF16),
            pltpu.VMEM((8, 1024, 256), BF16),
            pltpu.VMEM((1024, 3 * K), BF16),
            pltpu.VMEM((2048, K), F32),
            pltpu.VMEM((7, 256, K), F32),
            pltpu.VMEM((2048, K), F32),
            pltpu.VMEM((1024, K), F32),
            pltpu.VMEM((7, 128, K), F32),
            pltpu.VMEM((1024, K), F32),
            pltpu.VMEM((K, K), F32),
            pltpu.VMEM((7, 16, K), F32),
            pltpu.VMEM((K, K), F32),
            pltpu.VMEM((K, 2 * K), F32),
            pltpu.VMEM((K, K), F32),
            pltpu.VMEM((16, K), jnp.int32),
            pltpu.VMEM((8, 8, K), F32),
            pltpu.VMEM((256, K), F32),
            pltpu.VMEM((256, K), F32),
            pltpu.VMEM((1024, K), F32),
            pltpu.VMEM((1024, K), F32),
            pltpu.VMEM((K, K), F32),
            pltpu.VMEM((8, 64, K), F32),
            pltpu.VMEM((8, 64, K), F32),
            pltpu.VMEM((64, K), F32),
            pltpu.VMEM((64, K), F32),
            dma((2, 4)),
            dma((7,)), dma((7,)), dma((7,)), dma((7,)), dma((7,)), dma((7,)), dma((7,)), dma((7,)),
            dma((7,)), dma((7,)), dma((7,)), dma((7,)), dma((7,)), dma((7,)), dma((4,)), dma((4,)),
            dma((7,)), dma((7,)), dma((7,)), dma((7,)),
        ],
        compiler_params=pltpu.CompilerParams(
            collective_id=0, has_side_effects=True, vmem_limit_bytes=48 * 2**20
        ),
        name="subspace",
    )(activations, gradients, start_act, start_grad, doc_ids.reshape(8, 128))


def solution(mesh):
    placed = (P("dp", "feat"), P("dp", "feat"), P("feat", None), P("feat", None), P("dp"))
    return jax.shard_map(
        local,
        mesh=mesh,
        in_specs=placed,
        out_specs=(P("feat", None), P("feat", None), P()),
        check_vma=False,
    )
```

```python
import functools

import jax
import jax.numpy as jnp
from jax import lax
from jax.experimental import pallas as pl
from jax.experimental.pallas import tpu as pltpu
from jax.sharding import PartitionSpec as P

ITERS = 6
K = 128
MESH = pl.DeviceIdType.MESH
F32 = jnp.float32
BF16 = jnp.bfloat16
HIGHEST = lax.Precision.HIGHEST

OFFSETS = ((2, 1), (1, 1), (3, 1), (2, 0), (0, 1), (1, 0), (3, 0))


def pieces(value):
    high = value.astype(BF16)
    rest = value - high.astype(F32)
    mid = rest.astype(BF16)
    low = (rest - mid.astype(F32)).astype(BF16)
    return jnp.concatenate([high, mid, low], axis=1)


def joined(product):
    return product[:, :K] + (product[:, K : 2 * K] + product[:, 2 * K :])


def times(a, b):
    return lax.dot_general(a, b, (((1,), (0,)), ((), ())), preferred_element_type=F32)


def full(a, b, contract):
    return lax.dot_general(
        a, b, ((contract[:1], contract[1:]), ((), ())), precision=HIGHEST, preferred_element_type=F32
    )


def kernel(
    act_ref, grad_ref, start_act_ref, start_grad_ref, ids_ref,
    basis_act_ref, basis_grad_ref, scales_ref,
    x_send, x_recv, x, xt, split,
    y_send, y_recv, p, v_send, v_recv, v,
    g_send, g_recv, g, work, inverse,
    ids, c_recv, proj_mine, proj_other, basis_mine, basis_other,
    s_part, s_feat, s_dp, s_mine, s_other,
    x_sems, y_ssem, y_rsem, p_ssem, p_rsem, v_ssem, v_rsem, w_ssem, w_rsem,
    gs_ssem, gs_rsem, ga_ssem, ga_rsem, c_ssem, c_rsem, core_ssem, core_rsem,
    sf_ssem, sf_rsem, sd_ssem, sd_rsem,
):
    dp, feat = lax.axis_index("dp"), lax.axis_index("feat")
    core, q = dp % 2, dp // 2
    px, py = q % 4, q // 4
    fz, fy = feat // 2, feat % 2

    def feat_peer(r):
        dz, dy = OFFSETS[r]
        return ((fz + dz) % 4) * 2 + (fy + dy) % 2

    def feat_from(r):
        dz, dy = OFFSETS[r]
        return ((fz + 4 - dz) % 4) * 2 + (fy + dy) % 2

    def q_peer(r):
        dx, dy = OFFSETS[r]
        return ((py + dy) % 2) * 4 + (px + dx) % 4

    def q_from(r):
        dx, dy = OFFSETS[r]
        return ((py + dy) % 2) * 4 + (px + 4 - dx) % 4

    def to_feat(r, src, dst, ssem, rsem):
        return pltpu.make_async_remote_copy(
            src_ref=src, dst_ref=dst, send_sem=ssem.at[r], recv_sem=rsem.at[r],
            device_id={"feat": feat_peer(r)}, device_id_type=MESH,
        )

    def to_dp(r, src, dst, ssem, rsem):
        return pltpu.make_async_remote_copy(
            src_ref=src, dst_ref=dst, send_sem=ssem.at[r], recv_sem=rsem.at[r],
            device_id={"dp": q_peer(r) * 2 + core}, device_id_type=MESH,
        )

    def to_core(i, src, dst):
        return pltpu.make_async_remote_copy(
            src_ref=src, dst_ref=dst, send_sem=core_ssem.at[i], recv_sem=core_rsem.at[i],
            device_id={"dp": q * 2 + (1 - core)}, device_id_type=MESH,
        )

    barrier = pltpu.get_barrier_semaphore()
    for r in range(7):
        pl.semaphore_signal(barrier, inc=1, device_id={"feat": feat_peer(r)}, device_id_type=MESH)
        pl.semaphore_signal(
            barrier, inc=1, device_id={"dp": q_peer(r) * 2 + core}, device_id_type=MESH
        )
    pl.semaphore_signal(
        barrier, inc=1, device_id={"dp": q * 2 + (1 - core)}, device_id_type=MESH
    )
    pl.semaphore_wait(barrier, 15)

    even = core == 0
    ids_own = pl.ds(pl.multiple_of(core * 8, 8), 8)
    ids[ids_own, :] = ids_ref[...]
    ids_copy = to_core(0, ids.at[ids_own, :], ids.at[ids_own, :])
    ids_copy.start()
    x_copies = []
    for i in range(4):
        rows = slice(i * 256, (i + 1) * 256)
        x_send[rows, :] = jnp.where(even, grad_ref[rows, :].astype(F32), act_ref[rows, :].astype(F32))
        copy = pltpu.make_async_remote_copy(
            src_ref=x_send.at[rows, :], dst_ref=x_recv.at[rows, :],
            send_sem=x_sems.at[0, i], recv_sem=x_sems.at[1, i],
            device_id={"dp": q * 2 + (1 - core)}, device_id_type=MESH,
        )
        copy.start()
        x_copies.append(copy)
    for i in range(4):
        rows = slice(i * 256, (i + 1) * 256)
        x[pl.ds(pl.multiple_of(core * 1024 + i * 256, 256), 256), :] = jnp.where(
            even, act_ref[rows, :].astype(F32), grad_ref[rows, :].astype(F32)
        ).astype(BF16)
    v[...] = jnp.where(even, start_act_ref[...], start_grad_ref[...])
    lane = lax.broadcasted_iota(jnp.int32, (K, K), 1)
    row = lax.broadcasted_iota(jnp.int32, (K, K), 0)
    inverse[...] = (lane == row).astype(F32)
    for i in range(4):
        x_copies[i].wait()
        x[pl.ds(pl.multiple_of((1 - core) * 1024 + i * 256, 256), 256), :] = x_recv[
            i * 256 : (i + 1) * 256, :
        ].astype(BF16)

    def token_rows(f):
        return pl.ds(pl.multiple_of(f * 256, 256), 256)

    def gram_rows(f):
        return pl.ds(pl.multiple_of(f * 16, 16), 16)

    def half_rows(f, h):
        return pl.ds(pl.multiple_of(f * 256 + h * 128, 128), 128)

    def y_copy(r, h):
        return to_feat(
            r, y_send.at[half_rows(feat_peer(r), h), :], y_recv.at[r, h], y_ssem.at[h], y_rsem.at[h]
        )

    def project():
        split[...] = pieces(v[...])
        for r in range(7):
            rows = token_rows(feat_peer(r))
            y_send[rows, :] = joined(times(x[rows, :], split[...]))
            y_copy(r, 0).start()
        for r in range(7):
            y_copy(r, 1).start()
        rows = token_rows(feat)
        y_send[rows, :] = joined(times(x[rows, :], split[...]))

    def projected(h):
        for r in range(7):
            y_copy(r, h).wait()
        total = y_send[half_rows(feat, h), :]
        for r in range(7):
            total = total + y_recv[r, h]
        return total

    def gram_send():
        image = v[...]
        g_send[...] = full(image, image, (0, 0))
        copies = []
        for r in range(7):
            copy = to_feat(r, g_send.at[gram_rows(feat_peer(r)), :], g_recv.at[r], gs_ssem, gs_rsem)
            copy.start()
            copies.append(copy)
        return copies

    def gram_copies():
        return [
            to_feat(r, g_send.at[gram_rows(feat_peer(r)), :], g_recv.at[r], gs_ssem, gs_rsem)
            for r in range(7)
        ]

    def gram_gathers():
        mine = gram_rows(feat)
        return [to_feat(r, g.at[mine, :], g.at[mine, :], ga_ssem, ga_rsem) for r in range(7)]

    def gram_sum():
        for copy in gram_copies():
            copy.wait()
        total = g_send[gram_rows(feat), :]
        for r in range(7):
            total = total + g_recv[r]
        g[gram_rows(feat), :] = total
        for copy in gram_gathers():
            copy.start()

    def eliminate(first, last):
        small_row = lax.broadcasted_iota(jnp.int32, (8, K), 0)
        wide_row = lax.broadcasted_iota(jnp.int32, (K, 2 * K), 0)

        def panel(i, _):
            at = pl.ds(pl.multiple_of(i * 8, 8), 8)
            left, right = work[at, :K], work[at, K:]
            block = pltpu.roll(left, (K - i * 8) % K, 1)
            column = [jnp.broadcast_to(block[:, j : j + 1], (8, K)) for j in range(8)]
            pivots = jnp.ones((8, K), F32)
            for j in range(8):
                pivot = jnp.broadcast_to(column[j][j : j + 1, :], (8, K))
                ratio = jnp.where(small_row > j, column[j] * (1.0 / pivot), 0.0)
                pivots = jnp.where(small_row == j, pivot, pivots)
                for k in range(j + 1, 8):
                    column[k] = column[k] - ratio * column[k][j : j + 1, :]
                left = left - ratio * left[j : j + 1, :]
                right = right - ratio * right[j : j + 1, :]
            scale = lax.rsqrt(pivots)
            scale = scale * (1.5 - 0.5 * pivots * scale * scale)
            fresh = jnp.concatenate([left * scale, right * scale], axis=1)
            update = full(fresh[:, :K], fresh, (0, 0))
            work[...] = jnp.where(wide_row >= i * 8 + 8, work[...] - update, work[...])
            work[at, :] = fresh
            return 0

        lax.fori_loop(first, last, panel, 0)

    def factor_start():
        for copy in gram_gathers():
            copy.wait()
        work[:, :K] = g[...]
        work[:, K:] = (lane == row).astype(F32)
        eliminate(0, 8)

    def factor_end():
        eliminate(8, 16)
        inverse[...] = work[:, K:]

    def p_copy(r, h):
        mine = half_rows(feat, h)
        return to_feat(r, p.at[mine, :], p.at[mine, :], p_ssem.at[h], p_rsem.at[h])

    def v_copy(r, h):
        rows = part_rows(q_peer(r), h)
        return to_dp(r, v_send.at[rows, :], v_recv.at[r, h], v_ssem.at[h], v_rsem.at[h])

    def w_copy(r, h):
        mine = part_rows(q, h)
        return to_dp(r, v.at[mine, :], v.at[mine, :], w_ssem.at[h], w_rsem.at[h])

    def part_rows(i, h):
        return pl.ds(pl.multiple_of(i * 128 + h * 64, 64), 64)

    def sweep(step, _):
        project()

        @pl.when(step > 0)
        def _():
            gram_send()

        @pl.when(step == 0)
        def _():
            for c in range(16):
                xt[c] = x[c * 128 : (c + 1) * 128, :].T

        p[half_rows(feat, 0), :] = projected(0)

        @pl.when(step > 0)
        def _():
            gram_sum()

        for r in range(7):
            p_copy(r, 0).start()
        p[half_rows(feat, 1), :] = projected(1)
        for r in range(7):
            p_copy(r, 1).start()

        @pl.when(step > 0)
        def _():
            factor_start()

        for h in range(2):
            part = joined(times(xt[feat * 2 + h], pieces(p[half_rows(feat, h), :])))
            if h == 0:
                v_send[...] = part
            else:
                v_send[...] += part
            for r in reversed(range(7)):
                p_copy(r, h).wait()
                source = feat_from(r)
                v_send[...] += joined(
                    times(xt[source * 2 + h], pieces(p[half_rows(source, h), :]))
                )

        for h in range(2):
            for r in range(7):
                v_copy(r, h).start()

        @pl.when(step > 0)
        def _():
            factor_end()

        for h in range(2):
            for r in range(7):
                v_copy(r, h).wait()
            total = v_send[part_rows(q, h), :]
            for r in range(7):
                total = total + v_recv[r, h]
            v[part_rows(q, h), :] = full(total, inverse[...], (1, 1))
            for r in range(7):
                w_copy(r, h).start()
        for h in range(2):
            for r in range(7):
                w_copy(r, h).wait()
        return 0

    lax.fori_loop(0, ITERS, sweep, 0)

    project()
    gram_send()
    ids_copy.wait()
    counts = jnp.zeros((1, K), F32)
    for i in range(16):
        column = jnp.broadcast_to(ids[i : i + 1, :].astype(F32), (K, K)).T
        counts = counts + jnp.sum((column == lane.astype(F32)).astype(F32), axis=0, keepdims=True)
    c_recv[q] = jnp.broadcast_to(counts, (8, K))
    c_copies = [to_dp(r, c_recv.at[q], c_recv.at[q], c_ssem, c_rsem) for r in range(7)]
    for copy in c_copies:
        copy.start()

    gram_sum()
    total = jnp.concatenate([projected(0), projected(1)], axis=0)
    factor_start()
    factor_end()
    basis_mine[...] = full(v[...], inverse[...], (1, 1))
    proj_mine[...] = full(total, inverse[...], (1, 1))
    proj_copy = to_core(1, proj_mine, proj_other)
    proj_copy.start()
    basis_copy = to_core(2, basis_mine, basis_other)
    basis_copy.start()
    for copy in c_copies:
        copy.wait()
    counts = c_recv[0]
    for i in range(1, 8):
        counts = counts + c_recv[i]
    counts = counts[0:1, :]
    documents = 2 * lax.axis_size("dp")
    share = jnp.where(counts > 0, 1.0 / (documents * jnp.maximum(counts, 1.0)), 0.0)
    weight = []
    for i in range(2):
        column = jnp.broadcast_to(ids[pl.ds(feat * 2 + i, 1), :].astype(F32), (K, K)).T
        weight.append(
            jnp.sum(jnp.where(column == lane.astype(F32), share, 0.0), axis=1, keepdims=True)
        )
    proj_copy.wait()
    proj_act = jnp.where(even, proj_mine[...], proj_other[...])
    proj_grad = jnp.where(even, proj_other[...], proj_mine[...])
    left = jnp.concatenate(weight, axis=0) * proj_grad * proj_grad
    s_part[...] = full(left, proj_act * proj_act, (0, 0))

    half = pl.ds(pl.multiple_of(core * 64, 64), 64)
    s_feat[feat] = s_part[half, :]
    copies = [to_feat(r, s_feat.at[feat], s_feat.at[feat], sf_ssem, sf_rsem) for r in range(7)]
    for copy in copies:
        copy.start()
    for copy in copies:
        copy.wait()
    total = s_feat[0]
    for i in range(1, 8):
        total = total + s_feat[i]
    s_dp[q] = total
    copies = [to_dp(r, s_dp.at[q], s_dp.at[q], sd_ssem, sd_rsem) for r in range(7)]
    for copy in copies:
        copy.start()
    basis_copy.wait()
    basis_act_ref[...] = jnp.where(even, basis_mine[...], basis_other[...])
    basis_grad_ref[...] = jnp.where(even, basis_other[...], basis_mine[...])
    for copy in copies:
        copy.wait()
    total = s_dp[0]
    for i in range(1, 8):
        total = total + s_dp[i]
    s_mine[...] = total
    s_copy = to_core(3, s_mine, s_other)
    s_copy.start()
    s_copy.wait()
    scales_ref[half, :] = s_mine[...]
    scales_ref[pl.ds(pl.multiple_of((1 - core) * 64, 64), 64), :] = s_other[...]


def local(activations, gradients, start_act, start_grad, doc_ids):
    vmem = pl.BlockSpec(memory_space=pltpu.VMEM)
    dma = pltpu.SemaphoreType.DMA
    return pl.pallas_call(
        kernel,
        out_shape=(
            jax.ShapeDtypeStruct((1024, K), F32),
            jax.ShapeDtypeStruct((1024, K), F32),
            jax.ShapeDtypeStruct((K, K), F32),
        ),
        in_specs=[vmem] * 5,
        out_specs=(vmem,) * 3,
        scratch_shapes=[
            pltpu.VMEM((1024, 1024), F32),
            pltpu.VMEM((1024, 1024), F32),
            pltpu.VMEM((2048, 1024), BF16),
            pltpu.VMEM((16, 1024, 128), BF16),
            pltpu.VMEM((1024, 3 * K), BF16),
            pltpu.VMEM((2048, K), F32),
            pltpu.VMEM((7, 2, 128, K), F32),
            pltpu.VMEM((2048, K), F32),
            pltpu.VMEM((1024, K), F32),
            pltpu.VMEM((7, 2, 64, K), F32),
            pltpu.VMEM((1024, K), F32),
            pltpu.VMEM((K, K), F32),
            pltpu.VMEM((7, 16, K), F32),
            pltpu.VMEM((K, K), F32),
            pltpu.VMEM((K, 2 * K), F32),
            pltpu.VMEM((K, K), F32),
            pltpu.VMEM((16, K), jnp.int32),
            pltpu.VMEM((8, 8, K), F32),
            pltpu.VMEM((256, K), F32),
            pltpu.VMEM((256, K), F32),
            pltpu.VMEM((1024, K), F32),
            pltpu.VMEM((1024, K), F32),
            pltpu.VMEM((K, K), F32),
            pltpu.VMEM((8, 64, K), F32),
            pltpu.VMEM((8, 64, K), F32),
            pltpu.VMEM((64, K), F32),
            pltpu.VMEM((64, K), F32),
            dma((2, 4)),
            dma((2, 7)), dma((2, 7)), dma((2, 7)), dma((2, 7)),
            dma((2, 7)), dma((2, 7)), dma((2, 7)), dma((2, 7)),
            dma((7,)), dma((7,)), dma((7,)), dma((7,)), dma((7,)), dma((7,)), dma((4,)), dma((4,)),
            dma((7,)), dma((7,)), dma((7,)), dma((7,)),
        ],
        compiler_params=pltpu.CompilerParams(
            collective_id=0, has_side_effects=True, vmem_limit_bytes=48 * 2**20
        ),
        name="subspace",
    )(activations, gradients, start_act, start_grad, doc_ids.reshape(8, 128))


def solution(mesh):
    placed = (P("dp", "feat"), P("dp", "feat"), P("feat", None), P("feat", None), P("dp"))
    return jax.shard_map(
        local,
        mesh=mesh,
        in_specs=placed,
        out_specs=(P("feat", None), P("feat", None), P()),
        check_vma=False,
    )
```

```python
import functools

import jax
import jax.numpy as jnp
from jax import lax
from jax.experimental import pallas as pl
from jax.experimental.pallas import tpu as pltpu
from jax.sharding import PartitionSpec as P

ITERS = 6
K = 128
MESH = pl.DeviceIdType.MESH
F32 = jnp.float32
BF16 = jnp.bfloat16
HIGHEST = lax.Precision.HIGHEST

OFFSETS = ((2, 1), (1, 1), (3, 1), (2, 0), (0, 1), (1, 0), (3, 0))


def pieces(value):
    high = value.astype(BF16)
    low = (value - high.astype(F32)).astype(BF16)
    return jnp.concatenate([high, low], axis=1)


def joined(product):
    return product[:, :K] + product[:, K:]


def times(a, b):
    return lax.dot_general(a, b, (((1,), (0,)), ((), ())), preferred_element_type=F32)


def full(a, b, contract):
    return lax.dot_general(
        a, b, ((contract[:1], contract[1:]), ((), ())), precision=HIGHEST, preferred_element_type=F32
    )


def kernel(
    act_ref, grad_ref, start_act_ref, start_grad_ref, ids_ref,
    basis_act_ref, basis_grad_ref, scales_ref,
    x_send, x_recv, x, xt, split,
    y_send, y_recv, p, v_send, v_recv, v,
    g_send, g_recv, g, work, inverse,
    ids, c_recv, proj_mine, proj_other, basis_mine, basis_other,
    s_part, s_feat, s_dp, s_mine, s_other,
    x_sems, y_ssem, y_rsem, p_ssem, p_rsem, v_ssem, v_rsem, w_ssem, w_rsem,
    gs_ssem, gs_rsem, ga_ssem, ga_rsem, c_ssem, c_rsem, core_ssem, core_rsem,
    sf_ssem, sf_rsem, sd_ssem, sd_rsem,
):
    dp, feat = lax.axis_index("dp"), lax.axis_index("feat")
    core, q = dp % 2, dp // 2
    px, py = q % 4, q // 4
    fz, fy = feat // 2, feat % 2

    def feat_peer(r):
        dz, dy = OFFSETS[r]
        return ((fz + dz) % 4) * 2 + (fy + dy) % 2

    def feat_from(r):
        dz, dy = OFFSETS[r]
        return ((fz + 4 - dz) % 4) * 2 + (fy + dy) % 2

    def q_peer(r):
        dx, dy = OFFSETS[r]
        return ((py + dy) % 2) * 4 + (px + dx) % 4

    def q_from(r):
        dx, dy = OFFSETS[r]
        return ((py + dy) % 2) * 4 + (px + 4 - dx) % 4

    def to_feat(r, src, dst, ssem, rsem):
        return pltpu.make_async_remote_copy(
            src_ref=src, dst_ref=dst, send_sem=ssem.at[r], recv_sem=rsem.at[r],
            device_id={"feat": feat_peer(r)}, device_id_type=MESH,
        )

    def to_dp(r, src, dst, ssem, rsem):
        return pltpu.make_async_remote_copy(
            src_ref=src, dst_ref=dst, send_sem=ssem.at[r], recv_sem=rsem.at[r],
            device_id={"dp": q_peer(r) * 2 + core}, device_id_type=MESH,
        )

    def to_core(i, src, dst):
        return pltpu.make_async_remote_copy(
            src_ref=src, dst_ref=dst, send_sem=core_ssem.at[i], recv_sem=core_rsem.at[i],
            device_id={"dp": q * 2 + (1 - core)}, device_id_type=MESH,
        )

    barrier = pltpu.get_barrier_semaphore()
    for r in range(7):
        pl.semaphore_signal(barrier, inc=1, device_id={"feat": feat_peer(r)}, device_id_type=MESH)
        pl.semaphore_signal(
            barrier, inc=1, device_id={"dp": q_peer(r) * 2 + core}, device_id_type=MESH
        )
    pl.semaphore_signal(
        barrier, inc=1, device_id={"dp": q * 2 + (1 - core)}, device_id_type=MESH
    )
    pl.semaphore_wait(barrier, 15)

    even = core == 0
    ids[:8, :] = ids_ref[...]
    ids_copy = to_core(0, ids.at[:8, :], ids.at[8:, :])
    ids_copy.start()
    x_copies = []
    for i in range(4):
        rows = slice(i * 256, (i + 1) * 256)
        x_send[rows, :] = jnp.where(even, grad_ref[rows, :].astype(F32), act_ref[rows, :].astype(F32))
        copy = pltpu.make_async_remote_copy(
            src_ref=x_send.at[rows, :], dst_ref=x_recv.at[rows, :],
            send_sem=x_sems.at[0, i], recv_sem=x_sems.at[1, i],
            device_id={"dp": q * 2 + (1 - core)}, device_id_type=MESH,
        )
        copy.start()
        x_copies.append(copy)
    for i in range(4):
        rows = slice(i * 256, (i + 1) * 256)
        x[rows, :] = jnp.where(
            even, act_ref[rows, :].astype(F32), grad_ref[rows, :].astype(F32)
        ).astype(BF16)
    v[...] = jnp.where(even, start_act_ref[...], start_grad_ref[...])
    lane = lax.broadcasted_iota(jnp.int32, (K, K), 1)
    row = lax.broadcasted_iota(jnp.int32, (K, K), 0)
    inverse[...] = (lane == row).astype(F32)
    def half_rows(f, h):
        return pl.ds(pl.multiple_of(h * 1024 + f * 128, 128), 128)

    def pair_rows(j, h):
        return pl.ds(pl.multiple_of(h * 1024 + j * 256, 256), 256)

    def gram_rows(f):
        return pl.ds(pl.multiple_of(f * 16, 16), 16)

    def y_copy(r, h):
        return to_feat(
            r, y_send.at[half_rows(feat_peer(r), h), :], y_recv.at[r, h], y_ssem.at[h], y_rsem.at[h]
        )

    def project_half(h):
        rows = slice(h * 1024, (h + 1) * 1024)
        y_send[rows, :] = joined(times(x[rows, :], split[...]))
        for r in range(7):
            y_copy(r, h).start()

    def projected(h):
        for r in range(7):
            y_copy(r, h).wait()
        total = y_send[half_rows(feat, h), :]
        for r in range(7):
            total = total + y_recv[r, h]
        return total

    def gram_send():
        image = v[...]
        g_send[...] = full(image, image, (0, 0))
        for copy in gram_copies():
            copy.start()

    def gram_copies():
        return [
            to_feat(r, g_send.at[gram_rows(feat_peer(r)), :], g_recv.at[r], gs_ssem, gs_rsem)
            for r in range(7)
        ]

    def gram_gathers():
        mine = gram_rows(feat)
        return [to_feat(r, g.at[mine, :], g.at[mine, :], ga_ssem, ga_rsem) for r in range(7)]

    def gram_sum():
        for copy in gram_copies():
            copy.wait()
        total = g_send[gram_rows(feat), :]
        for r in range(7):
            total = total + g_recv[r]
        g[gram_rows(feat), :] = total
        for copy in gram_gathers():
            copy.start()

    def eliminate(first, last):
        small_row = lax.broadcasted_iota(jnp.int32, (8, K), 0)
        wide_row = lax.broadcasted_iota(jnp.int32, (K, 2 * K), 0)

        def panel(i, _):
            at = pl.ds(pl.multiple_of(i * 8, 8), 8)
            left, right = work[at, :K], work[at, K:]
            block = pltpu.roll(left, (K - i * 8) % K, 1)
            column = [jnp.broadcast_to(block[:, j : j + 1], (8, K)) for j in range(8)]
            pivots = jnp.ones((8, K), F32)
            for j in range(8):
                pivot = jnp.broadcast_to(column[j][j : j + 1, :], (8, K))
                ratio = jnp.where(small_row > j, column[j] * (1.0 / pivot), 0.0)
                pivots = jnp.where(small_row == j, pivot, pivots)
                for k in range(j + 1, 8):
                    column[k] = column[k] - ratio * column[k][j : j + 1, :]
                left = left - ratio * left[j : j + 1, :]
                right = right - ratio * right[j : j + 1, :]
            scale = lax.rsqrt(pivots)
            scale = scale * (1.5 - 0.5 * pivots * scale * scale)
            fresh = jnp.concatenate([left * scale, right * scale], axis=1)
            update = full(fresh[:, :K], fresh, (0, 0))
            work[...] = jnp.where(wide_row >= i * 8 + 8, work[...] - update, work[...])
            work[at, :] = fresh
            return 0

        lax.fori_loop(first, last, panel, 0)

    def factor_start():
        for copy in gram_gathers():
            copy.wait()
        work[:, :K] = g[...]
        work[:, K:] = (lane == row).astype(F32)
        eliminate(0, 5)

    def factor_end():
        eliminate(5, 16)
        inverse[...] = work[:, K:]

    def p_copy(r, h):
        mine = half_rows(feat, h)
        return to_feat(r, p.at[mine, :], p.at[mine, :], p_ssem.at[h], p_rsem.at[h])

    def v_copy(r, h):
        rows = part_rows(q_peer(r), h)
        return to_dp(r, v_send.at[rows, :], v_recv.at[r, h], v_ssem.at[h], v_rsem.at[h])

    def w_copy(r, h):
        mine = part_rows(q, h)
        return to_dp(r, v.at[mine, :], v.at[mine, :], w_ssem.at[h], w_rsem.at[h])

    def part_rows(i, h):
        return pl.ds(pl.multiple_of(i * 128 + h * 64, 64), 64)

    def c_copy(r):
        return to_dp(r, c_recv.at[q], c_recv.at[q], c_ssem, c_rsem)

    def count_documents():
        ids_copy.wait()
        counts = jnp.zeros((1, K), F32)
        for i in range(16):
            column = jnp.broadcast_to(ids[i : i + 1, :].astype(F32), (K, K)).T
            counts = counts + jnp.sum((column == lane.astype(F32)).astype(F32), axis=0, keepdims=True)
        c_recv[q] = jnp.broadcast_to(counts, (8, K))
        for r in range(7):
            c_copy(r).start()

    def receive_rest():
        for i in range(4):
            x_copies[i].wait()
            x[1024 + i * 256 : 1280 + i * 256, :] = x_recv[i * 256 : (i + 1) * 256, :].astype(BF16)

    def transpose():
        for c in range(8):
            xt[c] = x[c * 256 : (c + 1) * 256, :].T

    def sweep(step, _):
        split[...] = pieces(v[...])
        project_half(0)
        pl.when(step == 0)(receive_rest)
        project_half(1)
        pl.when(step > 0)(gram_send)

        @pl.when(step == 0)
        def _():
            transpose()
            count_documents()

        p[half_rows(feat, 0), :] = projected(0)
        for r in range(7):
            p_copy(r, 0).start()
        pl.when(step > 0)(gram_sum)
        p[half_rows(feat, 1), :] = projected(1)
        for r in range(7):
            p_copy(r, 1).start()

        for h in range(2):
            for dz in (0, 1, 3, 2):
                for r in range(7):
                    if OFFSETS[r][0] == dz:
                        p_copy(r, h).wait()
                j = (fz + 4 - dz) % 4
                part = joined(times(xt[h * 4 + j], pieces(p[pair_rows(j, h), :])))
                if h == 0 and dz == 0:
                    v_send[...] = part
                else:
                    v_send[...] += part
            if h == 0:
                pl.when(step > 0)(factor_start)

        for h in range(2):
            for r in range(7):
                v_copy(r, h).start()

        pl.when(step > 0)(factor_end)

        for h in range(2):
            for r in range(7):
                v_copy(r, h).wait()
            total = v_send[part_rows(q, h), :]
            for r in range(7):
                total = total + v_recv[r, h]
            v[part_rows(q, h), :] = full(total, inverse[...], (1, 1))
            for r in range(7):
                w_copy(r, h).start()
        for h in range(2):
            for r in range(7):
                w_copy(r, h).wait()
        return 0

    lax.fori_loop(0, ITERS, sweep, 0)

    gram_send()
    split[...] = pieces(v[...])
    project_half(0)
    project_half(1)
    gram_sum()
    for r in range(7):
        c_copy(r).wait()
    counts = c_recv[0]
    for i in range(1, 8):
        counts = counts + c_recv[i]
    counts = counts[0:1, :]
    documents = 2 * lax.axis_size("dp")
    share = jnp.where(counts > 0, 1.0 / (documents * jnp.maximum(counts, 1.0)), 0.0)
    weight = []
    for i in range(2):
        column = jnp.broadcast_to(ids[pl.ds(i * 8 + feat, 1), :].astype(F32), (K, K)).T
        weight.append(
            jnp.sum(jnp.where(column == lane.astype(F32), share, 0.0), axis=1, keepdims=True)
        )
    factor_start()
    factor_end()
    total = jnp.concatenate([projected(0), projected(1)], axis=0)
    proj_mine[...] = full(total, inverse[...], (1, 1))
    proj_copies = [
        to_core(i, proj_mine.at[mine, :], proj_other.at[theirs, :])
        for i, mine, theirs in ((1, slice(0, 128), slice(128, 256)), (4, slice(128, 256), slice(0, 128)))
    ]
    for copy in proj_copies:
        copy.start()
    basis_mine[...] = full(v[...], inverse[...], (1, 1))
    basis_copy = to_core(2, basis_mine, basis_other)
    basis_copy.start()
    for copy in proj_copies:
        copy.wait()
    proj_act = jnp.where(even, proj_mine[...], proj_other[...])
    proj_grad = jnp.where(even, proj_other[...], proj_mine[...])
    left = jnp.concatenate(weight, axis=0) * proj_grad * proj_grad
    s_part[...] = full(left, proj_act * proj_act, (0, 0))

    half = pl.ds(pl.multiple_of(core * 64, 64), 64)
    s_feat[feat] = s_part[half, :]
    copies = [to_feat(r, s_feat.at[feat], s_feat.at[feat], sf_ssem, sf_rsem) for r in range(7)]
    for copy in copies:
        copy.start()
    for copy in copies:
        copy.wait()
    total = s_feat[0]
    for i in range(1, 8):
        total = total + s_feat[i]
    s_dp[q] = total
    copies = [to_dp(r, s_dp.at[q], s_dp.at[q], sd_ssem, sd_rsem) for r in range(7)]
    for copy in copies:
        copy.start()
    basis_copy.wait()
    basis_act_ref[...] = jnp.where(even, basis_mine[...], basis_other[...])
    basis_grad_ref[...] = jnp.where(even, basis_other[...], basis_mine[...])
    for copy in copies:
        copy.wait()
    total = s_dp[0]
    for i in range(1, 8):
        total = total + s_dp[i]
    s_mine[...] = total
    s_copy = to_core(3, s_mine, s_other)
    s_copy.start()
    s_copy.wait()
    scales_ref[half, :] = s_mine[...]
    scales_ref[pl.ds(pl.multiple_of((1 - core) * 64, 64), 64), :] = s_other[...]


def local(activations, gradients, start_act, start_grad, doc_ids):
    vmem = pl.BlockSpec(memory_space=pltpu.VMEM)
    dma = pltpu.SemaphoreType.DMA
    return pl.pallas_call(
        kernel,
        out_shape=(
            jax.ShapeDtypeStruct((1024, K), F32),
            jax.ShapeDtypeStruct((1024, K), F32),
            jax.ShapeDtypeStruct((K, K), F32),
        ),
        in_specs=[vmem] * 5,
        out_specs=(vmem,) * 3,
        scratch_shapes=[
            pltpu.VMEM((1024, 1024), F32),
            pltpu.VMEM((1024, 1024), F32),
            pltpu.VMEM((2048, 1024), BF16),
            pltpu.VMEM((8, 1024, 256), BF16),
            pltpu.VMEM((1024, 2 * K), BF16),
            pltpu.VMEM((2048, K), F32),
            pltpu.VMEM((7, 2, 128, K), F32),
            pltpu.VMEM((2048, K), F32),
            pltpu.VMEM((1024, K), F32),
            pltpu.VMEM((7, 2, 64, K), F32),
            pltpu.VMEM((1024, K), F32),
            pltpu.VMEM((K, K), F32),
            pltpu.VMEM((7, 16, K), F32),
            pltpu.VMEM((K, K), F32),
            pltpu.VMEM((K, 2 * K), F32),
            pltpu.VMEM((K, K), F32),
            pltpu.VMEM((16, K), jnp.int32),
            pltpu.VMEM((8, 8, K), F32),
            pltpu.VMEM((256, K), F32),
            pltpu.VMEM((256, K), F32),
            pltpu.VMEM((1024, K), F32),
            pltpu.VMEM((1024, K), F32),
            pltpu.VMEM((K, K), F32),
            pltpu.VMEM((8, 64, K), F32),
            pltpu.VMEM((8, 64, K), F32),
            pltpu.VMEM((64, K), F32),
            pltpu.VMEM((64, K), F32),
            dma((2, 4)),
            dma((2, 7)), dma((2, 7)), dma((2, 7)), dma((2, 7)),
            dma((2, 7)), dma((2, 7)), dma((2, 7)), dma((2, 7)),
            dma((7,)), dma((7,)), dma((7,)), dma((7,)), dma((7,)), dma((7,)), dma((5,)), dma((5,)),
            dma((7,)), dma((7,)), dma((7,)), dma((7,)),
        ],
        compiler_params=pltpu.CompilerParams(
            collective_id=0, has_side_effects=True, vmem_limit_bytes=48 * 2**20
        ),
        name="subspace",
    )(activations, gradients, start_act, start_grad, doc_ids.reshape(8, 128))


def solution(mesh):
    placed = (P("dp", "feat"), P("dp", "feat"), P("feat", None), P("feat", None), P("dp"))
    return jax.shard_map(
        local,
        mesh=mesh,
        in_specs=placed,
        out_specs=(P("feat", None), P("feat", None), P()),
        check_vma=False,
    )
```

```python
import functools

import jax
import jax.numpy as jnp
from jax import lax
from jax.experimental import pallas as pl
from jax.experimental.pallas import tpu as pltpu
from jax.sharding import PartitionSpec as P

ITERS = 6
FIRST, SECOND = 6, 11
K = 128
MESH = pl.DeviceIdType.MESH
F32 = jnp.float32
BF16 = jnp.bfloat16
HIGHEST = lax.Precision.HIGHEST

OFFSETS = ((2, 1), (1, 1), (3, 1), (2, 0), (0, 1), (1, 0), (3, 0))


def pieces(value):
    high = value.astype(BF16)
    low = (value - high.astype(F32)).astype(BF16)
    return jnp.concatenate([high, low], axis=1)


def joined(product):
    return product[:, :K] + product[:, K:]


def times(a, b):
    return lax.dot_general(a, b, (((1,), (0,)), ((), ())), preferred_element_type=F32)


def full(a, b, contract):
    return lax.dot_general(
        a, b, ((contract[:1], contract[1:]), ((), ())), precision=HIGHEST, preferred_element_type=F32
    )


def kernel(
    act_ref, grad_ref, start_act_ref, start_grad_ref, ids_ref,
    basis_act_ref, basis_grad_ref, scales_ref,
    x_stage, x_send, x_recv, x, xt, split,
    y_send, y_recv, p, v_send, v_recv, v,
    g_send, g_recv, g_feat, g, work, inverse,
    ids, c_recv, proj_mine, proj_other, basis_mine, basis_other,
    s_part, s_feat, s_dp, s_mine, s_other,
    load_sems, x_sems, y_ssem, y_rsem, p_ssem, p_rsem, v_ssem, v_rsem, w_ssem, w_rsem,
    gs_ssem, gs_rsem, gf_ssem, gf_rsem, ga_ssem, ga_rsem, c_ssem, c_rsem, core_ssem, core_rsem,
    sf_ssem, sf_rsem, sd_ssem, sd_rsem,
):
    dp, feat = lax.axis_index("dp"), lax.axis_index("feat")
    core, q = dp % 2, dp // 2
    px, py = q % 4, q // 4
    fz, fy = feat // 2, feat % 2

    def feat_peer(r):
        dz, dy = OFFSETS[r]
        return ((fz + dz) % 4) * 2 + (fy + dy) % 2

    def feat_from(r):
        dz, dy = OFFSETS[r]
        return ((fz + 4 - dz) % 4) * 2 + (fy + dy) % 2

    def q_peer(r):
        dx, dy = OFFSETS[r]
        return ((py + dy) % 2) * 4 + (px + dx) % 4

    def q_from(r):
        dx, dy = OFFSETS[r]
        return ((py + dy) % 2) * 4 + (px + 4 - dx) % 4

    def to_feat(r, src, dst, ssem, rsem):
        return pltpu.make_async_remote_copy(
            src_ref=src, dst_ref=dst, send_sem=ssem.at[r], recv_sem=rsem.at[r],
            device_id={"feat": feat_peer(r)}, device_id_type=MESH,
        )

    def to_dp(r, src, dst, ssem, rsem):
        return pltpu.make_async_remote_copy(
            src_ref=src, dst_ref=dst, send_sem=ssem.at[r], recv_sem=rsem.at[r],
            device_id={"dp": q_peer(r) * 2 + core}, device_id_type=MESH,
        )

    def to_core(i, src, dst):
        return pltpu.make_async_remote_copy(
            src_ref=src, dst_ref=dst, send_sem=core_ssem.at[i], recv_sem=core_rsem.at[i],
            device_id={"dp": q * 2 + (1 - core)}, device_id_type=MESH,
        )

    barrier = pltpu.get_barrier_semaphore()
    for r in range(7):
        pl.semaphore_signal(barrier, inc=1, device_id={"feat": feat_peer(r)}, device_id_type=MESH)
        pl.semaphore_signal(
            barrier, inc=1, device_id={"dp": q_peer(r) * 2 + core}, device_id_type=MESH
        )
    pl.semaphore_signal(
        barrier, inc=1, device_id={"dp": q * 2 + (1 - core)}, device_id_type=MESH
    )

    even = core == 0

    def load(mine, theirs, start):
        own = [
            pltpu.make_async_copy(start, v, load_sems.at[0]),
            pltpu.make_async_copy(mine, x.at[:1024, :], load_sems.at[1]),
        ]
        other = [
            pltpu.make_async_copy(
                theirs.at[i * 256 : (i + 1) * 256, :],
                x_stage.at[i * 256 : (i + 1) * 256, :],
                load_sems.at[2 + i],
            )
            for i in range(4)
        ]
        for copy in other + own:
            copy.start()
        for i in range(4):
            rows = slice(i * 256, (i + 1) * 256)
            other[i].wait()
            x_send[rows, :] = x_stage[rows, :].astype(F32)
        for copy in own:
            copy.wait()

    pl.when(even)(lambda: load(act_ref, grad_ref, start_act_ref))
    pl.when(core == 1)(lambda: load(grad_ref, act_ref, start_grad_ref))
    ids[:8, :] = ids_ref[...]
    pl.semaphore_wait(barrier, 15)
    ids_copy = to_core(0, ids.at[:8, :], ids.at[8:, :])
    ids_copy.start()
    x_copies = []
    for i in range(4):
        rows = slice(i * 256, (i + 1) * 256)
        copy = pltpu.make_async_remote_copy(
            src_ref=x_send.at[rows, :], dst_ref=x_recv.at[rows, :],
            send_sem=x_sems.at[0, i], recv_sem=x_sems.at[1, i],
            device_id={"dp": q * 2 + (1 - core)}, device_id_type=MESH,
        )
        copy.start()
        x_copies.append(copy)
    lane = lax.broadcasted_iota(jnp.int32, (K, K), 1)
    row = lax.broadcasted_iota(jnp.int32, (K, K), 0)
    inverse[...] = (lane == row).astype(F32)
    def half_rows(f, h):
        return pl.ds(pl.multiple_of(h * 1024 + f * 128, 128), 128)

    def pair_rows(j, h):
        return pl.ds(pl.multiple_of(h * 1024 + j * 256, 256), 256)

    def gram_rows(i):
        return pl.ds(pl.multiple_of(i * 16, 16), 16)

    def y_copy(r, h):
        return to_feat(
            r, y_send.at[half_rows(feat_peer(r), h), :], y_recv.at[r, h], y_ssem.at[h], y_rsem.at[h]
        )

    def project_half(h, send):
        for dz in (2, 1, 3, 0):
            rows = pair_rows((fz + dz) % 4, h)
            y_send[rows, :] = joined(times(x[rows, :], split[...]))
            if send:
                for r in range(7):
                    if OFFSETS[r][0] == dz:
                        y_copy(r, h).start()

    def projected(h):
        for r in range(7):
            y_copy(r, h).wait()
        total = y_send[half_rows(feat, h), :]
        for r in range(7):
            total = total + y_recv[r, h]
        return total

    def gram_scatters():
        return [
            to_dp(r, g_send.at[gram_rows(q_peer(r)), :], g_recv.at[r], gs_ssem, gs_rsem)
            for r in range(7)
        ]

    def gram_swaps():
        return [to_feat(r, g_feat.at[feat], g_feat.at[feat], gf_ssem, gf_rsem) for r in range(7)]

    def gram_gathers():
        mine = gram_rows(q)
        return [to_dp(r, g.at[mine, :], g.at[mine, :], ga_ssem, ga_rsem) for r in range(7)]

    def gram_scatter():
        piece = v[pl.ds(pl.multiple_of(q * 128, 128), 128), :]
        g_send[...] = full(piece, piece, (0, 0))
        for copy in gram_scatters():
            copy.start()

    def gram_swap():
        for copy in gram_scatters():
            copy.wait()
        total = g_send[gram_rows(q), :]
        for r in range(7):
            total = total + g_recv[r]
        g_feat[feat] = total
        for copy in gram_swaps():
            copy.start()

    def gram_gather():
        for copy in gram_swaps():
            copy.wait()
        total = g_feat[0]
        for i in range(1, 8):
            total = total + g_feat[i]
        g[gram_rows(q), :] = total
        for copy in gram_gathers():
            copy.start()

    def eliminate(first, last):
        small_row = lax.broadcasted_iota(jnp.int32, (8, K), 0)
        wide_row = lax.broadcasted_iota(jnp.int32, (K, 2 * K), 0)

        def panel(i, _):
            at = pl.ds(pl.multiple_of(i * 8, 8), 8)
            left, right = work[at, :K], work[at, K:]
            block = pltpu.roll(left, (K - i * 8) % K, 1)
            column = [jnp.broadcast_to(block[:, j : j + 1], (8, K)) for j in range(8)]
            pivots = jnp.ones((8, K), F32)
            for j in range(8):
                pivot = jnp.broadcast_to(column[j][j : j + 1, :], (8, K))
                ratio = jnp.where(small_row > j, column[j] * (1.0 / pivot), 0.0)
                pivots = jnp.where(small_row == j, pivot, pivots)
                for k in range(j + 1, 8):
                    column[k] = column[k] - ratio * column[k][j : j + 1, :]
                left = left - ratio * left[j : j + 1, :]
                right = right - ratio * right[j : j + 1, :]
            scale = lax.rsqrt(pivots)
            scale = scale * (1.5 - 0.5 * pivots * scale * scale)
            fresh = jnp.concatenate([left * scale, right * scale], axis=1)
            update = full(fresh[:, :K], fresh, (0, 0))
            work[...] = jnp.where(wide_row >= i * 8 + 8, work[...] - update, work[...])
            work[at, :] = fresh
            return 0

        lax.fori_loop(first, last, panel, 0)

    def factor_start():
        for copy in gram_gathers():
            copy.wait()
        work[:, :K] = g[...]
        work[:, K:] = (lane == row).astype(F32)
        eliminate(0, FIRST)

    def factor_middle():
        eliminate(FIRST, SECOND)

    def factor_end():
        eliminate(SECOND, 16)
        inverse[...] = work[:, K:]

    def p_copy(r, h):
        mine = half_rows(feat, h)
        return to_feat(r, p.at[mine, :], p.at[mine, :], p_ssem.at[h], p_rsem.at[h])

    def v_copy(r, h):
        rows = part_rows(q_peer(r), h)
        return to_dp(r, v_send.at[rows, :], v_recv.at[r, h], v_ssem.at[h], v_rsem.at[h])

    def w_copy(r, h):
        mine = part_rows(q, h)
        return to_dp(r, v.at[mine, :], v.at[mine, :], w_ssem.at[h], w_rsem.at[h])

    def part_rows(i, h):
        return pl.ds(pl.multiple_of(i * 128 + h * 64, 64), 64)

    def c_copy(r):
        return to_dp(r, c_recv.at[q], c_recv.at[q], c_ssem, c_rsem)

    def count_documents():
        ids_copy.wait()
        counts = jnp.zeros((1, K), F32)
        for i in range(16):
            column = jnp.broadcast_to(ids[i : i + 1, :].astype(F32), (K, K)).T
            counts = counts + jnp.sum((column == lane.astype(F32)).astype(F32), axis=0, keepdims=True)
        c_recv[q] = jnp.broadcast_to(counts, (8, K))
        for r in range(7):
            c_copy(r).start()

    def receive_rest():
        for i in range(4):
            x_copies[i].wait()
            x[1024 + i * 256 : 1280 + i * 256, :] = x_recv[i * 256 : (i + 1) * 256, :].astype(BF16)

    def transpose():
        for c in range(8):
            xt[c] = x[c * 256 : (c + 1) * 256, :].T

    def sweep(step, _):
        split[...] = pieces(v[...])
        project_half(0, True)
        pl.when(step == 0)(receive_rest)
        project_half(1, True)
        pl.when(step > 0)(gram_gather)

        @pl.when(step == 0)
        def _():
            transpose()
            count_documents()

        p[half_rows(feat, 0), :] = projected(0)
        for r in range(7):
            p_copy(r, 0).start()
        p[half_rows(feat, 1), :] = projected(1)
        for r in range(7):
            p_copy(r, 1).start()

        pl.when(step > 0)(factor_start)
        for h in range(2):
            for dz in (0, 1, 3, 2):
                for r in range(7):
                    if OFFSETS[r][0] == dz:
                        p_copy(r, h).wait()
                j = (fz + 4 - dz) % 4
                part = joined(times(xt[h * 4 + j], pieces(p[pair_rows(j, h), :])))
                if h == 0 and dz == 0:
                    v_send[...] = part
                else:
                    v_send[...] += part
            if h == 0:
                pl.when(step > 0)(factor_middle)

        for h in range(2):
            for r in range(7):
                v_copy(r, h).start()

        pl.when(step > 0)(factor_end)

        for h in range(2):
            for r in range(7):
                v_copy(r, h).wait()
            total = v_send[part_rows(q, h), :]
            for r in range(7):
                total = total + v_recv[r, h]
            v[part_rows(q, h), :] = full(total, inverse[...], (1, 1))
            for r in range(7):
                w_copy(r, h).start()
        gram_scatter()
        for h in range(2):
            for r in range(7):
                w_copy(r, h).wait()
        gram_swap()
        return 0

    lax.fori_loop(0, ITERS, sweep, 0)

    split[...] = pieces(v[...])
    project_half(0, True)
    project_half(1, False)
    gram_gather()
    for r in range(7):
        y_copy(r, 1).start()
    for r in range(7):
        c_copy(r).wait()
    counts = c_recv[0]
    for i in range(1, 8):
        counts = counts + c_recv[i]
    counts = counts[0:1, :]
    documents = 2 * lax.axis_size("dp")
    share = jnp.where(counts > 0, 1.0 / (documents * jnp.maximum(counts, 1.0)), 0.0)
    weight = []
    for i in range(2):
        column = jnp.broadcast_to(ids[pl.ds(i * 8 + feat, 1), :].astype(F32), (K, K)).T
        weight.append(
            jnp.sum(jnp.where(column == lane.astype(F32), share, 0.0), axis=1, keepdims=True)
        )
    factor_start()
    factor_middle()
    factor_end()
    total = jnp.concatenate([projected(0), projected(1)], axis=0)
    proj_mine[...] = full(total, inverse[...], (1, 1))
    proj_copies = [
        to_core(i, proj_mine.at[mine, :], proj_other.at[theirs, :])
        for i, mine, theirs in ((1, slice(0, 128), slice(128, 256)), (4, slice(128, 256), slice(0, 128)))
    ]
    for copy in proj_copies:
        copy.start()
    basis_mine[...] = full(v[...], inverse[...], (1, 1))
    basis_copy = to_core(2, basis_mine, basis_other)
    basis_copy.start()
    for copy in proj_copies:
        copy.wait()
    proj_act = jnp.where(even, proj_mine[...], proj_other[...])
    proj_grad = jnp.where(even, proj_other[...], proj_mine[...])
    left = jnp.concatenate(weight, axis=0) * proj_grad * proj_grad
    s_part[...] = full(left, proj_act * proj_act, (0, 0))

    half = pl.ds(pl.multiple_of(core * 64, 64), 64)
    s_feat[feat] = s_part[half, :]
    copies = [to_feat(r, s_feat.at[feat], s_feat.at[feat], sf_ssem, sf_rsem) for r in range(7)]
    for copy in copies:
        copy.start()
    for copy in copies:
        copy.wait()
    total = s_feat[0]
    for i in range(1, 8):
        total = total + s_feat[i]
    s_dp[q] = total
    copies = [to_dp(r, s_dp.at[q], s_dp.at[q], sd_ssem, sd_rsem) for r in range(7)]
    for copy in copies:
        copy.start()
    basis_copy.wait()
    basis_act_ref[...] = jnp.where(even, basis_mine[...], basis_other[...])
    basis_grad_ref[...] = jnp.where(even, basis_other[...], basis_mine[...])
    for copy in copies:
        copy.wait()
    total = s_dp[0]
    for i in range(1, 8):
        total = total + s_dp[i]
    s_mine[...] = total
    s_copy = to_core(3, s_mine, s_other)
    s_copy.start()
    s_copy.wait()
    scales_ref[half, :] = s_mine[...]
    scales_ref[pl.ds(pl.multiple_of((1 - core) * 64, 64), 64), :] = s_other[...]


def local(activations, gradients, start_act, start_grad, doc_ids):
    vmem = pl.BlockSpec(memory_space=pltpu.VMEM)
    hbm = pl.BlockSpec(memory_space=pl.ANY)
    dma = pltpu.SemaphoreType.DMA
    return pl.pallas_call(
        kernel,
        out_shape=(
            jax.ShapeDtypeStruct((1024, K), F32),
            jax.ShapeDtypeStruct((1024, K), F32),
            jax.ShapeDtypeStruct((K, K), F32),
        ),
        in_specs=[hbm] * 4 + [vmem],
        out_specs=(vmem,) * 3,
        scratch_shapes=[
            pltpu.VMEM((1024, 1024), BF16),
            pltpu.VMEM((1024, 1024), F32),
            pltpu.VMEM((1024, 1024), F32),
            pltpu.VMEM((2048, 1024), BF16),
            pltpu.VMEM((8, 1024, 256), BF16),
            pltpu.VMEM((1024, 2 * K), BF16),
            pltpu.VMEM((2048, K), F32),
            pltpu.VMEM((7, 2, 128, K), F32),
            pltpu.VMEM((2048, K), F32),
            pltpu.VMEM((1024, K), F32),
            pltpu.VMEM((7, 2, 64, K), F32),
            pltpu.VMEM((1024, K), F32),
            pltpu.VMEM((K, K), F32),
            pltpu.VMEM((7, 16, K), F32),
            pltpu.VMEM((8, 16, K), F32),
            pltpu.VMEM((K, K), F32),
            pltpu.VMEM((K, 2 * K), F32),
            pltpu.VMEM((K, K), F32),
            pltpu.VMEM((16, K), jnp.int32),
            pltpu.VMEM((8, 8, K), F32),
            pltpu.VMEM((256, K), F32),
            pltpu.VMEM((256, K), F32),
            pltpu.VMEM((1024, K), F32),
            pltpu.VMEM((1024, K), F32),
            pltpu.VMEM((K, K), F32),
            pltpu.VMEM((8, 64, K), F32),
            pltpu.VMEM((8, 64, K), F32),
            pltpu.VMEM((64, K), F32),
            pltpu.VMEM((64, K), F32),
            dma((6,)), dma((2, 4)),
            dma((2, 7)), dma((2, 7)), dma((2, 7)), dma((2, 7)),
            dma((2, 7)), dma((2, 7)), dma((2, 7)), dma((2, 7)),
            dma((7,)), dma((7,)), dma((7,)), dma((7,)), dma((7,)), dma((7,)), dma((7,)), dma((7,)),
            dma((5,)), dma((5,)),
            dma((7,)), dma((7,)), dma((7,)), dma((7,)),
        ],
        compiler_params=pltpu.CompilerParams(
            collective_id=0, has_side_effects=True, vmem_limit_bytes=60 * 2**20
        ),
        name="subspace",
    )(activations, gradients, start_act, start_grad, doc_ids.reshape(8, 128))


def solution(mesh):
    placed = (P("dp", "feat"), P("dp", "feat"), P("feat", None), P("feat", None), P("dp"))
    return jax.shard_map(
        local,
        mesh=mesh,
        in_specs=placed,
        out_specs=(P("feat", None), P("feat", None), P()),
        check_vma=False,
    )
```

```python
import functools

import jax
import jax.numpy as jnp
from jax import lax
from jax.experimental import pallas as pl
from jax.experimental.pallas import tpu as pltpu
from jax.sharding import PartitionSpec as P

ITERS = 6
FIRST, SECOND = 3, 5
K = 128
MESH = pl.DeviceIdType.MESH
F32 = jnp.float32
BF16 = jnp.bfloat16
HIGHEST = lax.Precision.HIGHEST

OFFSETS = ((2, 1), (1, 1), (3, 1), (2, 0), (0, 1), (1, 0), (3, 0))


def pieces(value):
    high = value.astype(BF16)
    low = (value - high.astype(F32)).astype(BF16)
    return jnp.concatenate([high, low], axis=1)


def joined(product):
    return product[:, :K] + product[:, K:]


def times(a, b):
    return lax.dot_general(a, b, (((1,), (0,)), ((), ())), preferred_element_type=F32)


def full(a, b, contract):
    return lax.dot_general(
        a, b, ((contract[:1], contract[1:]), ((), ())), precision=HIGHEST, preferred_element_type=F32
    )


def kernel(
    act_ref, grad_ref, start_act_ref, start_grad_ref, ids_ref,
    basis_act_ref, basis_grad_ref, scales_ref,
    x_stage, x_send, x_recv, x, xt, split,
    y_send, y_recv, p, v_send, v_recv, v,
    g_send, g_recv, g_feat, g, work, inverse,
    ids, c_recv, proj_mine, proj_other, basis_mine, basis_other,
    s_part, s_feat, s_dp, s_mine, s_other,
    load_sems, x_sems, y_ssem, y_rsem, p_ssem, p_rsem, v_ssem, v_rsem, w_ssem, w_rsem,
    gs_ssem, gs_rsem, gf_ssem, gf_rsem, ga_ssem, ga_rsem, c_ssem, c_rsem, core_ssem, core_rsem,
    sf_ssem, sf_rsem, sd_ssem, sd_rsem, late_sem,
):
    dp, feat = lax.axis_index("dp"), lax.axis_index("feat")
    core, q = dp % 2, dp // 2
    px, py = q % 4, q // 4
    fz, fy = feat // 2, feat % 2

    def feat_peer(r):
        dz, dy = OFFSETS[r]
        return ((fz + dz) % 4) * 2 + (fy + dy) % 2

    def feat_from(r):
        dz, dy = OFFSETS[r]
        return ((fz + 4 - dz) % 4) * 2 + (fy + dy) % 2

    def q_peer(r):
        dx, dy = OFFSETS[r]
        return ((py + dy) % 2) * 4 + (px + dx) % 4

    def q_from(r):
        dx, dy = OFFSETS[r]
        return ((py + dy) % 2) * 4 + (px + 4 - dx) % 4

    def to_feat(r, src, dst, ssem, rsem):
        return pltpu.make_async_remote_copy(
            src_ref=src, dst_ref=dst, send_sem=ssem.at[r], recv_sem=rsem.at[r],
            device_id={"feat": feat_peer(r)}, device_id_type=MESH,
        )

    def to_dp(r, src, dst, ssem, rsem):
        return pltpu.make_async_remote_copy(
            src_ref=src, dst_ref=dst, send_sem=ssem.at[r], recv_sem=rsem.at[r],
            device_id={"dp": q_peer(r) * 2 + core}, device_id_type=MESH,
        )

    def to_core(i, src, dst):
        return pltpu.make_async_remote_copy(
            src_ref=src, dst_ref=dst, send_sem=core_ssem.at[i], recv_sem=core_rsem.at[i],
            device_id={"dp": q * 2 + (1 - core)}, device_id_type=MESH,
        )

    barrier = pltpu.get_barrier_semaphore()
    for r in range(7):
        pl.semaphore_signal(barrier, inc=1, device_id={"feat": feat_peer(r)}, device_id_type=MESH)
        pl.semaphore_signal(
            barrier, inc=1, device_id={"dp": q_peer(r) * 2 + core}, device_id_type=MESH
        )
    pl.semaphore_signal(
        barrier, inc=1, device_id={"dp": q * 2 + (1 - core)}, device_id_type=MESH
    )

    even = core == 0

    def load(mine, theirs, start):
        own = [
            pltpu.make_async_copy(start, v, load_sems.at[0]),
            pltpu.make_async_copy(mine, x.at[:1024, :], load_sems.at[1]),
        ]
        other = [
            pltpu.make_async_copy(
                theirs.at[i * 256 : (i + 1) * 256, :],
                x_stage.at[i * 256 : (i + 1) * 256, :],
                load_sems.at[2 + i],
            )
            for i in range(4)
        ]
        for copy in other + own:
            copy.start()
        for i in range(4):
            rows = slice(i * 256, (i + 1) * 256)
            other[i].wait()
            x_send[rows, :] = x_stage[rows, :].astype(F32)
        for copy in own:
            copy.wait()

    pl.when(even)(lambda: load(act_ref, grad_ref, start_act_ref))
    pl.when(core == 1)(lambda: load(grad_ref, act_ref, start_grad_ref))
    ids[:8, :] = ids_ref[...]
    pl.semaphore_wait(barrier, 15)
    ids_copy = to_core(0, ids.at[:8, :], ids.at[8:, :])
    ids_copy.start()
    x_copies = []
    for i in range(4):
        rows = slice(i * 256, (i + 1) * 256)
        copy = pltpu.make_async_remote_copy(
            src_ref=x_send.at[rows, :], dst_ref=x_recv.at[rows, :],
            send_sem=x_sems.at[0, i], recv_sem=x_sems.at[1, i],
            device_id={"dp": q * 2 + (1 - core)}, device_id_type=MESH,
        )
        copy.start()
        x_copies.append(copy)
    lane = lax.broadcasted_iota(jnp.int32, (K, K), 1)
    row = lax.broadcasted_iota(jnp.int32, (K, K), 0)
    inverse[...] = (lane == row).astype(F32)
    def half_rows(f, h):
        return pl.ds(pl.multiple_of(h * 1024 + f * 128, 128), 128)

    def pair_rows(j, h):
        return pl.ds(pl.multiple_of(h * 1024 + j * 256, 256), 256)

    def gram_rows(i):
        return pl.ds(pl.multiple_of(i * 16, 16), 16)

    def y_copy(r, h):
        return to_feat(
            r, y_send.at[half_rows(feat_peer(r), h), :], y_recv.at[r, h], y_ssem.at[h], y_rsem.at[h]
        )

    def project_half(h, send):
        for dz in (2, 1, 3, 0):
            rows = pair_rows((fz + dz) % 4, h)
            y_send[rows, :] = joined(times(x[rows, :], split[...]))
            if send:
                for r in range(7):
                    if OFFSETS[r][0] == dz:
                        y_copy(r, h).start()

    def projected(h):
        for r in range(7):
            y_copy(r, h).wait()
        total = y_send[half_rows(feat, h), :]
        for r in range(7):
            total = total + y_recv[r, h]
        return total

    def gram_scatters():
        return [
            to_dp(r, g_send.at[gram_rows(q_peer(r)), :], g_recv.at[r], gs_ssem, gs_rsem)
            for r in range(7)
        ]

    def gram_swaps():
        return [to_feat(r, g_feat.at[feat], g_feat.at[feat], gf_ssem, gf_rsem) for r in range(7)]

    def gram_gathers():
        mine = gram_rows(q)
        return [to_dp(r, g.at[mine, :], g.at[mine, :], ga_ssem, ga_rsem) for r in range(7)]

    def gram_scatter():
        piece = v[pl.ds(pl.multiple_of(q * 128, 128), 128), :]
        g_send[...] = full(piece, piece, (0, 0))
        for copy in gram_scatters():
            copy.start()

    def gram_swap():
        for copy in gram_scatters():
            copy.wait()
        total = g_send[gram_rows(q), :]
        for r in range(7):
            total = total + g_recv[r]
        g_feat[feat] = total
        for copy in gram_swaps():
            copy.start()

    def gram_gather():
        for copy in gram_swaps():
            copy.wait()
        total = g_feat[0]
        for i in range(1, 8):
            total = total + g_feat[i]
        g[gram_rows(q), :] = total
        for copy in gram_gathers():
            copy.start()

    def eliminate(first, last):
        small_row = lax.broadcasted_iota(jnp.int32, (16, K), 0)
        wide_row = lax.broadcasted_iota(jnp.int32, (K, 2 * K), 0)

        def panel(i, _):
            at = pl.ds(pl.multiple_of(i * 16, 16), 16)
            left, right = work[at, :K], work[at, K:]
            block = pltpu.roll(left, (K - i * 16) % K, 1)
            column = [jnp.broadcast_to(block[:, j : j + 1], (16, K)) for j in range(16)]
            pivots = jnp.ones((16, K), F32)
            for j in range(16):
                pivot = jnp.broadcast_to(column[j][j : j + 1, :], (16, K))
                ratio = jnp.where(small_row > j, column[j] * (1.0 / pivot), 0.0)
                pivots = jnp.where(small_row == j, pivot, pivots)
                for k in range(j + 1, 16):
                    column[k] = column[k] - ratio * column[k][j : j + 1, :]
                left = left - ratio * left[j : j + 1, :]
                right = right - ratio * right[j : j + 1, :]
            scale = lax.rsqrt(pivots)
            scale = scale * (1.5 - 0.5 * pivots * scale * scale)
            fresh = jnp.concatenate([left * scale, right * scale], axis=1)
            update = full(fresh[:, :K], fresh, (0, 0))
            work[...] = jnp.where(wide_row >= i * 16 + 16, work[...] - update, work[...])
            work[at, :] = fresh
            return 0

        lax.fori_loop(first, last, panel, 0)

    def factor_start():
        for copy in gram_gathers():
            copy.wait()
        work[:, :K] = g[...]
        work[:, K:] = (lane == row).astype(F32)
        eliminate(0, FIRST)

    def factor_middle():
        eliminate(FIRST, SECOND)

    def factor_end():
        eliminate(SECOND, 8)
        inverse[...] = work[:, K:]

    def p_copy(r, h):
        mine = half_rows(feat, h)
        return to_feat(r, p.at[mine, :], p.at[mine, :], p_ssem.at[h], p_rsem.at[h])

    def v_copy(r, h):
        rows = part_rows(q_peer(r), h)
        return to_dp(r, v_send.at[rows, :], v_recv.at[r, h], v_ssem.at[h], v_rsem.at[h])

    def w_copy(r, h):
        mine = part_rows(q, h)
        return to_dp(r, v.at[mine, :], v.at[mine, :], w_ssem.at[h], w_rsem.at[h])

    def part_rows(i, h):
        return pl.ds(pl.multiple_of(i * 128 + h * 64, 64), 64)

    def c_copy(r):
        return to_dp(r, c_recv.at[q], c_recv.at[q], c_ssem, c_rsem)

    def count_documents():
        ids_copy.wait()
        counts = jnp.zeros((1, K), F32)
        for i in range(16):
            column = jnp.broadcast_to(ids[i : i + 1, :].astype(F32), (K, K)).T
            counts = counts + jnp.sum((column == lane.astype(F32)).astype(F32), axis=0, keepdims=True)
        c_recv[q] = jnp.broadcast_to(counts, (8, K))
        for r in range(7):
            c_copy(r).start()

    def receive_rest():
        for i in range(4):
            x_copies[i].wait()
            x[1024 + i * 256 : 1280 + i * 256, :] = x_recv[i * 256 : (i + 1) * 256, :].astype(BF16)

    def transpose(h):
        for c in range(4 * h, 4 * h + 4):
            xt[c] = x[c * 256 : (c + 1) * 256, :].T

    def sweep(step, _):
        split[...] = pieces(v[...])

        @pl.when((step == 0) & (core == 1))
        def _():
            pl.semaphore_wait(late_sem, 1)

        project_half(0, True)

        @pl.when(step == 0)
        def _():
            transpose(0)
            receive_rest()

        project_half(1, True)
        pl.when(step > 0)(gram_gather)

        p[half_rows(feat, 0), :] = projected(0)
        for r in range(7):
            p_copy(r, 0).start()
        p[half_rows(feat, 1), :] = projected(1)
        for r in range(7):
            p_copy(r, 1).start()

        pl.when(step > 0)(factor_start)

        @pl.when(step == 0)
        def _():
            transpose(1)
            count_documents()

        for h in range(2):
            for dz in (0, 1, 3, 2):
                for r in range(7):
                    if OFFSETS[r][0] == dz:
                        p_copy(r, h).wait()
                j = (fz + 4 - dz) % 4
                part = joined(times(xt[h * 4 + j], pieces(p[pair_rows(j, h), :])))
                if h == 0 and dz == 0:
                    v_send[...] = part
                else:
                    v_send[...] += part
            if h == 0:
                pl.when(step > 0)(factor_middle)

        @pl.when((step == 0) & (core == 0))
        def _():
            pl.semaphore_signal(late_sem, inc=1, device_id={"dp": q * 2 + 1}, device_id_type=MESH)

        for h in range(2):
            for r in range(7):
                v_copy(r, h).start()

        pl.when(step > 0)(factor_end)

        for h in range(2):
            for r in range(7):
                v_copy(r, h).wait()
            total = v_send[part_rows(q, h), :]
            for r in range(7):
                total = total + v_recv[r, h]
            v[part_rows(q, h), :] = full(total, inverse[...], (1, 1))
            for r in range(7):
                w_copy(r, h).start()
        gram_scatter()
        for h in range(2):
            for r in range(7):
                w_copy(r, h).wait()
        gram_swap()
        return 0

    lax.fori_loop(0, ITERS, sweep, 0)

    split[...] = pieces(v[...])
    project_half(0, True)
    project_half(1, False)
    gram_gather()
    for r in range(7):
        y_copy(r, 1).start()
    for r in range(7):
        c_copy(r).wait()
    counts = c_recv[0]
    for i in range(1, 8):
        counts = counts + c_recv[i]
    counts = counts[0:1, :]
    documents = 2 * lax.axis_size("dp")
    share = jnp.where(counts > 0, 1.0 / (documents * jnp.maximum(counts, 1.0)), 0.0)
    weight = []
    for i in range(2):
        column = jnp.broadcast_to(ids[pl.ds(i * 8 + feat, 1), :].astype(F32), (K, K)).T
        weight.append(
            jnp.sum(jnp.where(column == lane.astype(F32), share, 0.0), axis=1, keepdims=True)
        )
    factor_start()
    factor_middle()
    factor_end()
    total = jnp.concatenate([projected(0), projected(1)], axis=0)
    proj_mine[...] = full(total, inverse[...], (1, 1))
    proj_copies = [
        to_core(i, proj_mine.at[mine, :], proj_other.at[theirs, :])
        for i, mine, theirs in ((1, slice(0, 128), slice(128, 256)), (4, slice(128, 256), slice(0, 128)))
    ]
    for copy in proj_copies:
        copy.start()
    for copy in proj_copies:
        copy.wait()
    proj_act = jnp.where(even, proj_mine[...], proj_other[...])
    proj_grad = jnp.where(even, proj_other[...], proj_mine[...])
    left = jnp.concatenate(weight, axis=0) * proj_grad * proj_grad
    s_part[...] = full(left, proj_act * proj_act, (0, 0))

    half = pl.ds(pl.multiple_of(core * 64, 64), 64)
    s_feat[feat] = s_part[half, :]
    copies = [to_feat(r, s_feat.at[feat], s_feat.at[feat], sf_ssem, sf_rsem) for r in range(7)]
    for copy in copies:
        copy.start()
    basis_mine[...] = full(v[...], inverse[...], (1, 1))
    basis_copy = to_core(2, basis_mine, basis_other)
    basis_copy.start()
    for copy in copies:
        copy.wait()
    total = s_feat[0]
    for i in range(1, 8):
        total = total + s_feat[i]
    s_dp[q] = total
    copies = [to_dp(r, s_dp.at[q], s_dp.at[q], sd_ssem, sd_rsem) for r in range(7)]
    for copy in copies:
        copy.start()
    basis_copy.wait()
    basis_act_ref[...] = jnp.where(even, basis_mine[...], basis_other[...])
    basis_grad_ref[...] = jnp.where(even, basis_other[...], basis_mine[...])
    for copy in copies:
        copy.wait()
    total = s_dp[0]
    for i in range(1, 8):
        total = total + s_dp[i]
    s_mine[...] = total
    s_copy = to_core(3, s_mine, s_other)
    s_copy.start()
    s_copy.wait()
    scales_ref[half, :] = s_mine[...]
    scales_ref[pl.ds(pl.multiple_of((1 - core) * 64, 64), 64), :] = s_other[...]


def local(activations, gradients, start_act, start_grad, doc_ids):
    vmem = pl.BlockSpec(memory_space=pltpu.VMEM)
    hbm = pl.BlockSpec(memory_space=pl.ANY)
    dma = pltpu.SemaphoreType.DMA
    return pl.pallas_call(
        kernel,
        out_shape=(
            jax.ShapeDtypeStruct((1024, K), F32),
            jax.ShapeDtypeStruct((1024, K), F32),
            jax.ShapeDtypeStruct((K, K), F32),
        ),
        in_specs=[hbm] * 4 + [vmem],
        out_specs=(vmem,) * 3,
        scratch_shapes=[
            pltpu.VMEM((1024, 1024), BF16),
            pltpu.VMEM((1024, 1024), F32),
            pltpu.VMEM((1024, 1024), F32),
            pltpu.VMEM((2048, 1024), BF16),
            pltpu.VMEM((8, 1024, 256), BF16),
            pltpu.VMEM((1024, 2 * K), BF16),
            pltpu.VMEM((2048, K), F32),
            pltpu.VMEM((7, 2, 128, K), F32),
            pltpu.VMEM((2048, K), F32),
            pltpu.VMEM((1024, K), F32),
            pltpu.VMEM((7, 2, 64, K), F32),
            pltpu.VMEM((1024, K), F32),
            pltpu.VMEM((K, K), F32),
            pltpu.VMEM((7, 16, K), F32),
            pltpu.VMEM((8, 16, K), F32),
            pltpu.VMEM((K, K), F32),
            pltpu.VMEM((K, 2 * K), F32),
            pltpu.VMEM((K, K), F32),
            pltpu.VMEM((16, K), jnp.int32),
            pltpu.VMEM((8, 8, K), F32),
            pltpu.VMEM((256, K), F32),
            pltpu.VMEM((256, K), F32),
            pltpu.VMEM((1024, K), F32),
            pltpu.VMEM((1024, K), F32),
            pltpu.VMEM((K, K), F32),
            pltpu.VMEM((8, 64, K), F32),
            pltpu.VMEM((8, 64, K), F32),
            pltpu.VMEM((64, K), F32),
            pltpu.VMEM((64, K), F32),
            dma((6,)), dma((2, 4)),
            dma((2, 7)), dma((2, 7)), dma((2, 7)), dma((2, 7)),
            dma((2, 7)), dma((2, 7)), dma((2, 7)), dma((2, 7)),
            dma((7,)), dma((7,)), dma((7,)), dma((7,)), dma((7,)), dma((7,)), dma((7,)), dma((7,)),
            dma((5,)), dma((5,)),
            dma((7,)), dma((7,)), dma((7,)), dma((7,)), pltpu.SemaphoreType.REGULAR,
        ],
        compiler_params=pltpu.CompilerParams(
            collective_id=0, has_side_effects=True, vmem_limit_bytes=60 * 2**20
        ),
        name="subspace",
    )(activations, gradients, start_act, start_grad, doc_ids.reshape(8, 128))


def solution(mesh):
    placed = (P("dp", "feat"), P("dp", "feat"), P("feat", None), P("feat", None), P("dp"))
    return jax.shard_map(
        local,
        mesh=mesh,
        in_specs=placed,
        out_specs=(P("feat", None), P("feat", None), P()),
        check_vma=False,
    )
```

```python
import functools

import jax
import jax.numpy as jnp
from jax import lax
from jax.experimental import pallas as pl
from jax.experimental.pallas import tpu as pltpu
from jax.sharding import PartitionSpec as P

ITERS = 6
FIRST, SECOND = 3, 5
K = 128
MESH = pl.DeviceIdType.MESH
F32 = jnp.float32
BF16 = jnp.bfloat16
HIGHEST = lax.Precision.HIGHEST

OFFSETS = ((2, 1), (1, 1), (3, 1), (2, 0), (0, 1), (1, 0), (3, 0))


def pieces(value):
    high = value.astype(BF16)
    low = (value - high.astype(F32)).astype(BF16)
    return jnp.concatenate([high, low], axis=1)


def joined(product):
    return product[:, :K] + product[:, K:]


def times(a, b):
    return lax.dot_general(a, b, (((1,), (0,)), ((), ())), preferred_element_type=F32)


def full(a, b, contract):
    return lax.dot_general(
        a, b, ((contract[:1], contract[1:]), ((), ())), precision=HIGHEST, preferred_element_type=F32
    )


def kernel(
    act_ref, grad_ref, start_act_ref, start_grad_ref, ids_ref,
    basis_act_ref, basis_grad_ref, scales_ref,
    x_stage, x_send, x_recv, x, xt, split,
    y_send, y_recv, p, v_send, v_recv, v,
    g_send, g_recv, g_feat, g, work, inverse,
    ids, c_recv, proj_mine, proj_other, basis_mine, basis_other,
    s_part, s_feat, s_dp, s_mine, s_other,
    load_sems, x_sems, y_ssem, y_rsem, p_ssem, p_rsem, v_ssem, v_rsem, w_ssem, w_rsem,
    gs_ssem, gs_rsem, gf_ssem, gf_rsem, ga_ssem, ga_rsem, c_ssem, c_rsem, core_ssem, core_rsem,
    sf_ssem, sf_rsem, sd_ssem, sd_rsem, late_sem,
):
    dp, feat = lax.axis_index("dp"), lax.axis_index("feat")
    core, q = dp % 2, dp // 2
    px, py = q % 4, q // 4
    fz, fy = feat // 2, feat % 2

    def feat_peer(r):
        dz, dy = OFFSETS[r]
        return ((fz + dz) % 4) * 2 + (fy + dy) % 2

    def feat_from(r):
        dz, dy = OFFSETS[r]
        return ((fz + 4 - dz) % 4) * 2 + (fy + dy) % 2

    def q_peer(r):
        dx, dy = OFFSETS[r]
        return ((py + dy) % 2) * 4 + (px + dx) % 4

    def q_from(r):
        dx, dy = OFFSETS[r]
        return ((py + dy) % 2) * 4 + (px + 4 - dx) % 4

    def to_feat(r, src, dst, ssem, rsem):
        return pltpu.make_async_remote_copy(
            src_ref=src, dst_ref=dst, send_sem=ssem.at[r], recv_sem=rsem.at[r],
            device_id={"feat": feat_peer(r)}, device_id_type=MESH,
        )

    def to_dp(r, src, dst, ssem, rsem):
        return pltpu.make_async_remote_copy(
            src_ref=src, dst_ref=dst, send_sem=ssem.at[r], recv_sem=rsem.at[r],
            device_id={"dp": q_peer(r) * 2 + core}, device_id_type=MESH,
        )

    def to_core(i, src, dst):
        return pltpu.make_async_remote_copy(
            src_ref=src, dst_ref=dst, send_sem=core_ssem.at[i], recv_sem=core_rsem.at[i],
            device_id={"dp": q * 2 + (1 - core)}, device_id_type=MESH,
        )

    barrier = pltpu.get_barrier_semaphore()
    for r in range(7):
        pl.semaphore_signal(barrier, inc=1, device_id={"feat": feat_peer(r)}, device_id_type=MESH)
        pl.semaphore_signal(
            barrier, inc=1, device_id={"dp": q_peer(r) * 2 + core}, device_id_type=MESH
        )
    pl.semaphore_signal(
        barrier, inc=1, device_id={"dp": q * 2 + (1 - core)}, device_id_type=MESH
    )

    even = core == 0

    def load(mine, theirs, start):
        own = [
            pltpu.make_async_copy(start, v, load_sems.at[0]),
            pltpu.make_async_copy(mine, x.at[:1024, :], load_sems.at[1]),
        ]
        other = [
            pltpu.make_async_copy(
                theirs.at[i * 256 : (i + 1) * 256, :],
                x_stage.at[i * 256 : (i + 1) * 256, :],
                load_sems.at[2 + i],
            )
            for i in range(4)
        ]
        for copy in other + own:
            copy.start()
        for i in range(4):
            rows = slice(i * 256, (i + 1) * 256)
            other[i].wait()
            x_send[rows, :] = x_stage[rows, :].astype(F32)
        for copy in own:
            copy.wait()

    ids_load = pltpu.make_async_copy(ids_ref, ids.at[:8, :], load_sems.at[6])
    ids_load.start()
    pl.when(even)(lambda: load(act_ref, grad_ref, start_act_ref))
    pl.when(core == 1)(lambda: load(grad_ref, act_ref, start_grad_ref))
    ids_load.wait()
    pl.semaphore_wait(barrier, 15)
    ids_copy = to_core(0, ids.at[:8, :], ids.at[8:, :])
    ids_copy.start()
    x_copies = []
    for i in range(4):
        rows = slice(i * 256, (i + 1) * 256)
        copy = pltpu.make_async_remote_copy(
            src_ref=x_send.at[rows, :], dst_ref=x_recv.at[rows, :],
            send_sem=x_sems.at[0, i], recv_sem=x_sems.at[1, i],
            device_id={"dp": q * 2 + (1 - core)}, device_id_type=MESH,
        )
        copy.start()
        x_copies.append(copy)
    lane = lax.broadcasted_iota(jnp.int32, (K, K), 1)
    row = lax.broadcasted_iota(jnp.int32, (K, K), 0)
    inverse[...] = (lane == row).astype(F32)
    def half_rows(f, h):
        return pl.ds(pl.multiple_of(h * 1024 + f * 128, 128), 128)

    def pair_rows(j, h):
        return pl.ds(pl.multiple_of(h * 1024 + j * 256, 256), 256)

    def gram_rows(i):
        return pl.ds(pl.multiple_of(i * 16, 16), 16)

    def y_copy(r, h):
        return to_feat(
            r, y_send.at[half_rows(feat_peer(r), h), :], y_recv.at[r, h], y_ssem.at[h], y_rsem.at[h]
        )

    def project_half(h, send):
        for dz in (2, 1, 3, 0):
            rows = pair_rows((fz + dz) % 4, h)
            y_send[rows, :] = joined(times(x[rows, :], split[...]))
            if send:
                for r in range(7):
                    if OFFSETS[r][0] == dz:
                        y_copy(r, h).start()

    def projected(h):
        for r in range(7):
            y_copy(r, h).wait()
        total = y_send[half_rows(feat, h), :]
        for r in range(7):
            total = total + y_recv[r, h]
        return total

    def gram_scatters():
        return [
            to_dp(r, g_send.at[gram_rows(q_peer(r)), :], g_recv.at[r], gs_ssem, gs_rsem)
            for r in range(7)
        ]

    def gram_swaps():
        return [to_feat(r, g_feat.at[feat], g_feat.at[feat], gf_ssem, gf_rsem) for r in range(7)]

    def gram_gathers():
        mine = gram_rows(q)
        return [to_dp(r, g.at[mine, :], g.at[mine, :], ga_ssem, ga_rsem) for r in range(7)]

    def gram_scatter():
        piece = v[pl.ds(pl.multiple_of(q * 128, 128), 128), :]
        g_send[...] = full(piece, piece, (0, 0))
        for copy in gram_scatters():
            copy.start()

    def gram_swap():
        for copy in gram_scatters():
            copy.wait()
        total = g_send[gram_rows(q), :]
        for r in range(7):
            total = total + g_recv[r]
        g_feat[feat] = total
        for copy in gram_swaps():
            copy.start()

    def gram_gather():
        for copy in gram_swaps():
            copy.wait()
        total = g_feat[0]
        for i in range(1, 8):
            total = total + g_feat[i]
        g[gram_rows(q), :] = total
        for copy in gram_gathers():
            copy.start()

    def eliminate(first, last):
        small_row = lax.broadcasted_iota(jnp.int32, (16, K), 0)
        wide_row = lax.broadcasted_iota(jnp.int32, (K, 2 * K), 0)

        def panel(i, _):
            at = pl.ds(pl.multiple_of(i * 16, 16), 16)
            left, right = work[at, :K], work[at, K:]
            block = pltpu.roll(left, (K - i * 16) % K, 1)
            column = [jnp.broadcast_to(block[:, j : j + 1], (16, K)) for j in range(16)]
            pivots = jnp.ones((16, K), F32)
            for j in range(16):
                pivot = jnp.broadcast_to(column[j][j : j + 1, :], (16, K))
                ratio = jnp.where(small_row > j, column[j] * (1.0 / pivot), 0.0)
                pivots = jnp.where(small_row == j, pivot, pivots)
                for k in range(j + 1, 16):
                    column[k] = column[k] - ratio * column[k][j : j + 1, :]
                left = left - ratio * left[j : j + 1, :]
                right = right - ratio * right[j : j + 1, :]
            scale = lax.rsqrt(pivots)
            scale = scale * (1.5 - 0.5 * pivots * scale * scale)
            fresh = jnp.concatenate([left * scale, right * scale], axis=1)
            update = full(fresh[:, :K], fresh, (0, 0))
            work[...] = jnp.where(wide_row >= i * 16 + 16, work[...] - update, work[...])
            work[at, :] = fresh
            return 0

        lax.fori_loop(first, last, panel, 0)

    def factor_start():
        for copy in gram_gathers():
            copy.wait()
        work[:, :K] = g[...]
        work[:, K:] = (lane == row).astype(F32)
        eliminate(0, FIRST)

    def factor_middle():
        eliminate(FIRST, SECOND)

    def factor_end():
        eliminate(SECOND, 8)
        inverse[...] = work[:, K:]

    def p_copy(r, h):
        mine = half_rows(feat, h)
        return to_feat(r, p.at[mine, :], p.at[mine, :], p_ssem.at[h], p_rsem.at[h])

    def v_copy(r, h):
        rows = part_rows(q_peer(r), h)
        return to_dp(r, v_send.at[rows, :], v_recv.at[r, h], v_ssem.at[h], v_rsem.at[h])

    def w_copy(r, h):
        mine = part_rows(q, h)
        return to_dp(r, v.at[mine, :], v.at[mine, :], w_ssem.at[h], w_rsem.at[h])

    def part_rows(i, h):
        return pl.ds(pl.multiple_of(i * 128 + h * 64, 64), 64)

    def c_copy(r):
        return to_dp(r, c_recv.at[q], c_recv.at[q], c_ssem, c_rsem)

    def count_documents():
        ids_copy.wait()
        counts = jnp.zeros((1, K), F32)
        for i in range(16):
            column = jnp.broadcast_to(ids[i : i + 1, :].astype(F32), (K, K)).T
            counts = counts + jnp.sum((column == lane.astype(F32)).astype(F32), axis=0, keepdims=True)
        c_recv[q] = jnp.broadcast_to(counts, (8, K))
        for r in range(7):
            c_copy(r).start()

    def receive_rest():
        for i in range(4):
            x_copies[i].wait()
            x[1024 + i * 256 : 1280 + i * 256, :] = x_recv[i * 256 : (i + 1) * 256, :].astype(BF16)

    def transpose(h):
        for c in range(4 * h, 4 * h + 4):
            xt[c] = x[c * 256 : (c + 1) * 256, :].T

    def sweep(step, _):
        split[...] = pieces(v[...])
        pl.when(step > 0)(gram_swap)

        @pl.when((step == 0) & (core == 1))
        def _():
            pl.semaphore_wait(late_sem, 1)

        project_half(0, True)

        @pl.when(step == 0)
        def _():
            transpose(0)
            receive_rest()

        project_half(1, True)
        pl.when(step > 0)(gram_gather)

        p[half_rows(feat, 0), :] = projected(0)
        for r in range(7):
            p_copy(r, 0).start()
        p[half_rows(feat, 1), :] = projected(1)
        for r in range(7):
            p_copy(r, 1).start()

        pl.when(step > 0)(factor_start)

        @pl.when(step == 0)
        def _():
            transpose(1)
            count_documents()

        for h in range(2):
            for dz in (0, 1, 3, 2):
                for r in range(7):
                    if OFFSETS[r][0] == dz:
                        p_copy(r, h).wait()
                j = (fz + 4 - dz) % 4
                part = joined(times(xt[h * 4 + j], pieces(p[pair_rows(j, h), :])))
                if h == 0 and dz == 0:
                    v_send[...] = part
                else:
                    v_send[...] += part
            if h == 0:
                pl.when(step > 0)(factor_middle)

        @pl.when((step == 0) & (core == 0))
        def _():
            pl.semaphore_signal(late_sem, inc=1, device_id={"dp": q * 2 + 1}, device_id_type=MESH)

        for h in range(2):
            for r in range(7):
                v_copy(r, h).start()

        pl.when(step > 0)(factor_end)

        for h in range(2):
            for r in range(7):
                v_copy(r, h).wait()
            total = v_send[part_rows(q, h), :]
            for r in range(7):
                total = total + v_recv[r, h]
            v[part_rows(q, h), :] = full(total, inverse[...], (1, 1))
            for r in range(7):
                w_copy(r, h).start()
        gram_scatter()
        for h in range(2):
            for r in range(7):
                w_copy(r, h).wait()
        return 0

    lax.fori_loop(0, ITERS, sweep, 0)

    split[...] = pieces(v[...])
    gram_swap()
    project_half(0, True)
    project_half(1, False)
    gram_gather()
    for r in range(7):
        y_copy(r, 1).start()
    for r in range(7):
        c_copy(r).wait()
    counts = c_recv[0]
    for i in range(1, 8):
        counts = counts + c_recv[i]
    counts = counts[0:1, :]
    documents = 2 * lax.axis_size("dp")
    share = jnp.where(counts > 0, 1.0 / (documents * jnp.maximum(counts, 1.0)), 0.0)
    weight = []
    for i in range(2):
        column = jnp.broadcast_to(ids[pl.ds(i * 8 + feat, 1), :].astype(F32), (K, K)).T
        weight.append(
            jnp.sum(jnp.where(column == lane.astype(F32), share, 0.0), axis=1, keepdims=True)
        )
    factor_start()
    factor_middle()
    factor_end()
    total = jnp.concatenate([projected(0), projected(1)], axis=0)
    proj_mine[...] = full(total, inverse[...], (1, 1))
    proj_copies = [
        to_core(i, proj_mine.at[mine, :], proj_other.at[theirs, :])
        for i, mine, theirs in ((1, slice(0, 128), slice(128, 256)), (4, slice(128, 256), slice(0, 128)))
    ]
    for copy in proj_copies:
        copy.start()
    for copy in proj_copies:
        copy.wait()
    proj_act = jnp.where(even, proj_mine[...], proj_other[...])
    proj_grad = jnp.where(even, proj_other[...], proj_mine[...])
    left = jnp.concatenate(weight, axis=0) * proj_grad * proj_grad
    s_part[...] = full(left, proj_act * proj_act, (0, 0))

    half = pl.ds(pl.multiple_of(core * 64, 64), 64)
    s_feat[feat] = s_part[half, :]
    copies = [to_feat(r, s_feat.at[feat], s_feat.at[feat], sf_ssem, sf_rsem) for r in range(7)]
    for copy in copies:
        copy.start()
    basis_mine[...] = full(v[...], inverse[...], (1, 1))
    basis_copy = to_core(2, basis_mine, basis_other)
    basis_copy.start()
    for copy in copies:
        copy.wait()
    total = s_feat[0]
    for i in range(1, 8):
        total = total + s_feat[i]
    s_dp[q] = total
    copies = [to_dp(r, s_dp.at[q], s_dp.at[q], sd_ssem, sd_rsem) for r in range(7)]
    for copy in copies:
        copy.start()
    basis_copy.wait()
    basis_act_ref[...] = jnp.where(even, basis_mine[...], basis_other[...])
    basis_grad_ref[...] = jnp.where(even, basis_other[...], basis_mine[...])
    for copy in copies:
        copy.wait()
    total = s_dp[0]
    for i in range(1, 8):
        total = total + s_dp[i]
    s_mine[...] = total
    s_copy = to_core(3, s_mine, s_other)
    s_copy.start()
    s_copy.wait()
    scales_ref[half, :] = s_mine[...]
    scales_ref[pl.ds(pl.multiple_of((1 - core) * 64, 64), 64), :] = s_other[...]


def local(activations, gradients, start_act, start_grad, doc_ids):
    vmem = pl.BlockSpec(memory_space=pltpu.VMEM)
    hbm = pl.BlockSpec(memory_space=pl.ANY)
    dma = pltpu.SemaphoreType.DMA
    return pl.pallas_call(
        kernel,
        out_shape=(
            jax.ShapeDtypeStruct((1024, K), F32),
            jax.ShapeDtypeStruct((1024, K), F32),
            jax.ShapeDtypeStruct((K, K), F32),
        ),
        in_specs=[hbm] * 5,
        out_specs=(vmem,) * 3,
        scratch_shapes=[
            pltpu.VMEM((1024, 1024), BF16),
            pltpu.VMEM((1024, 1024), F32),
            pltpu.VMEM((1024, 1024), F32),
            pltpu.VMEM((2048, 1024), BF16),
            pltpu.VMEM((8, 1024, 256), BF16),
            pltpu.VMEM((1024, 2 * K), BF16),
            pltpu.VMEM((2048, K), F32),
            pltpu.VMEM((7, 2, 128, K), F32),
            pltpu.VMEM((2048, K), F32),
            pltpu.VMEM((1024, K), F32),
            pltpu.VMEM((7, 2, 64, K), F32),
            pltpu.VMEM((1024, K), F32),
            pltpu.VMEM((K, K), F32),
            pltpu.VMEM((7, 16, K), F32),
            pltpu.VMEM((8, 16, K), F32),
            pltpu.VMEM((K, K), F32),
            pltpu.VMEM((K, 2 * K), F32),
            pltpu.VMEM((K, K), F32),
            pltpu.VMEM((16, K), jnp.int32),
            pltpu.VMEM((8, 8, K), F32),
            pltpu.VMEM((256, K), F32),
            pltpu.VMEM((256, K), F32),
            pltpu.VMEM((1024, K), F32),
            pltpu.VMEM((1024, K), F32),
            pltpu.VMEM((K, K), F32),
            pltpu.VMEM((8, 64, K), F32),
            pltpu.VMEM((8, 64, K), F32),
            pltpu.VMEM((64, K), F32),
            pltpu.VMEM((64, K), F32),
            dma((7,)), dma((2, 4)),
            dma((2, 7)), dma((2, 7)), dma((2, 7)), dma((2, 7)),
            dma((2, 7)), dma((2, 7)), dma((2, 7)), dma((2, 7)),
            dma((7,)), dma((7,)), dma((7,)), dma((7,)), dma((7,)), dma((7,)), dma((7,)), dma((7,)),
            dma((5,)), dma((5,)),
            dma((7,)), dma((7,)), dma((7,)), dma((7,)), pltpu.SemaphoreType.REGULAR,
        ],
        compiler_params=pltpu.CompilerParams(
            collective_id=0, has_side_effects=True, vmem_limit_bytes=50 * 2**20
        ),
        name="subspace",
    )(activations, gradients, start_act, start_grad, doc_ids.reshape(8, 128))


def solution(mesh):
    placed = (P("dp", "feat"), P("dp", "feat"), P("feat", None), P("feat", None), P("dp"))
    return jax.shard_map(
        local,
        mesh=mesh,
        in_specs=placed,
        out_specs=(P("feat", None), P("feat", None), P()),
        check_vma=False,
    )
```

```python
import functools

import jax
import jax.numpy as jnp
from jax import lax
from jax.experimental import pallas as pl
from jax.experimental.pallas import tpu as pltpu
from jax.sharding import PartitionSpec as P

ITERS = 6
FIRST, SECOND = 3, 5
K = 128
MESH = pl.DeviceIdType.MESH
F32 = jnp.float32
BF16 = jnp.bfloat16
HIGHEST = lax.Precision.HIGHEST

OFFSETS = ((2, 1), (1, 1), (3, 1), (0, 1), (2, 0), (1, 0), (3, 0))


def pieces(value):
    high = value.astype(BF16)
    low = (value - high.astype(F32)).astype(BF16)
    return jnp.concatenate([high, low], axis=1)


def joined(product):
    return product[:, :K] + product[:, K:]


def times(a, b):
    return lax.dot_general(a, b, (((1,), (0,)), ((), ())), preferred_element_type=F32)


def full(a, b, contract):
    return lax.dot_general(
        a, b, ((contract[:1], contract[1:]), ((), ())), precision=HIGHEST, preferred_element_type=F32
    )


def kernel(
    act_ref, grad_ref, start_act_ref, start_grad_ref, ids_ref,
    basis_act_ref, basis_grad_ref, scales_ref,
    x_stage, x_send, x_recv, x, xt, split,
    y_send, y_recv, p, v_send, v_recv, v,
    g_send, g_recv, g_feat, g, work, inverse,
    ids, c_recv, proj_mine, proj_other, basis_mine, basis_other,
    s_part, s_feat, s_dp, s_mine, s_other,
    load_sems, x_sems, y_ssem, y_rsem, p_ssem, p_rsem, v_ssem, v_rsem, w_ssem, w_rsem,
    gs_ssem, gs_rsem, gf_ssem, gf_rsem, ga_ssem, ga_rsem, c_ssem, c_rsem, core_ssem, core_rsem,
    sf_ssem, sf_rsem, sd_ssem, sd_rsem, late_sem,
):
    dp, feat = lax.axis_index("dp"), lax.axis_index("feat")
    core, q = dp % 2, dp // 2
    px, py = q % 4, q // 4
    fz, fy = feat // 2, feat % 2

    def feat_peer(r):
        dz, dy = OFFSETS[r]
        return ((fz + dz) % 4) * 2 + (fy + dy) % 2

    def feat_from(r):
        dz, dy = OFFSETS[r]
        return ((fz + 4 - dz) % 4) * 2 + (fy + dy) % 2

    def q_peer(r):
        dx, dy = OFFSETS[r]
        return ((py + dy) % 2) * 4 + (px + dx) % 4

    def q_from(r):
        dx, dy = OFFSETS[r]
        return ((py + dy) % 2) * 4 + (px + 4 - dx) % 4

    def to_feat(r, src, dst, ssem, rsem):
        return pltpu.make_async_remote_copy(
            src_ref=src, dst_ref=dst, send_sem=ssem.at[r], recv_sem=rsem.at[r],
            device_id={"feat": feat_peer(r)}, device_id_type=MESH,
        )

    def to_dp(r, src, dst, ssem, rsem):
        return pltpu.make_async_remote_copy(
            src_ref=src, dst_ref=dst, send_sem=ssem.at[r], recv_sem=rsem.at[r],
            device_id={"dp": q_peer(r) * 2 + core}, device_id_type=MESH,
        )

    def to_core(i, src, dst):
        return pltpu.make_async_remote_copy(
            src_ref=src, dst_ref=dst, send_sem=core_ssem.at[i], recv_sem=core_rsem.at[i],
            device_id={"dp": q * 2 + (1 - core)}, device_id_type=MESH,
        )

    barrier = pltpu.get_barrier_semaphore()
    for r in range(7):
        pl.semaphore_signal(barrier, inc=1, device_id={"feat": feat_peer(r)}, device_id_type=MESH)
        pl.semaphore_signal(
            barrier, inc=1, device_id={"dp": q_peer(r) * 2 + core}, device_id_type=MESH
        )
    pl.semaphore_signal(
        barrier, inc=1, device_id={"dp": q * 2 + (1 - core)}, device_id_type=MESH
    )

    even = core == 0

    def load(mine, theirs, start):
        own = [
            pltpu.make_async_copy(start, v, load_sems.at[0]),
            pltpu.make_async_copy(mine, x.at[:1024, :], load_sems.at[1]),
        ]
        other = [
            pltpu.make_async_copy(
                theirs.at[i * 256 : (i + 1) * 256, :],
                x_stage.at[i * 256 : (i + 1) * 256, :],
                load_sems.at[2 + i],
            )
            for i in range(4)
        ]
        for copy in other + own:
            copy.start()
        for i in range(4):
            rows = slice(i * 256, (i + 1) * 256)
            other[i].wait()
            x_send[rows, :] = x_stage[rows, :].astype(F32)
        for copy in own:
            copy.wait()

    ids_load = pltpu.make_async_copy(ids_ref, ids.at[:8, :], load_sems.at[6])
    ids_load.start()
    pl.when(even)(lambda: load(act_ref, grad_ref, start_act_ref))
    pl.when(core == 1)(lambda: load(grad_ref, act_ref, start_grad_ref))
    ids_load.wait()
    pl.semaphore_wait(barrier, 15)
    ids_copy = to_core(0, ids.at[:8, :], ids.at[8:, :])
    ids_copy.start()
    x_copies = []
    for i in range(4):
        rows = slice(i * 256, (i + 1) * 256)
        copy = pltpu.make_async_remote_copy(
            src_ref=x_send.at[rows, :], dst_ref=x_recv.at[rows, :],
            send_sem=x_sems.at[0, i], recv_sem=x_sems.at[1, i],
            device_id={"dp": q * 2 + (1 - core)}, device_id_type=MESH,
        )
        copy.start()
        x_copies.append(copy)
    lane = lax.broadcasted_iota(jnp.int32, (K, K), 1)
    row = lax.broadcasted_iota(jnp.int32, (K, K), 0)
    inverse[...] = (lane == row).astype(F32)
    def half_rows(f, h):
        return pl.ds(pl.multiple_of(h * 1024 + f * 128, 128), 128)

    def pair_rows(j, h):
        return pl.ds(pl.multiple_of(h * 1024 + j * 256, 256), 256)

    def gram_rows(i):
        return pl.ds(pl.multiple_of(i * 16, 16), 16)

    def y_copy(r, h):
        return to_feat(
            r, y_send.at[half_rows(feat_peer(r), h), :], y_recv.at[r, h], y_ssem.at[h], y_rsem.at[h]
        )

    def project_half(h, send):
        for dz in (2, 1, 3, 0):
            rows = pair_rows((fz + dz) % 4, h)
            y_send[rows, :] = joined(times(x[rows, :], split[...]))
            if send:
                for r in range(7):
                    if OFFSETS[r][0] == dz:
                        y_copy(r, h).start()

    def projected(h):
        for r in range(7):
            y_copy(r, h).wait()
        total = y_send[half_rows(feat, h), :]
        for r in range(7):
            total = total + y_recv[r, h]
        return total

    def gram_scatters():
        return [
            to_dp(r, g_send.at[gram_rows(q_peer(r)), :], g_recv.at[r], gs_ssem, gs_rsem)
            for r in range(7)
        ]

    def gram_swaps():
        return [to_feat(r, g_feat.at[feat], g_feat.at[feat], gf_ssem, gf_rsem) for r in range(7)]

    def gram_gathers():
        mine = gram_rows(q)
        return [to_dp(r, g.at[mine, :], g.at[mine, :], ga_ssem, ga_rsem) for r in range(7)]

    def gram_scatter():
        piece = v[pl.ds(pl.multiple_of(q * 128, 128), 128), :]
        g_send[...] = full(piece, piece, (0, 0))
        for copy in gram_scatters():
            copy.start()

    def gram_swap():
        for copy in gram_scatters():
            copy.wait()
        total = g_send[gram_rows(q), :]
        for r in range(7):
            total = total + g_recv[r]
        g_feat[feat] = total
        for copy in gram_swaps():
            copy.start()

    def gram_gather():
        for copy in gram_swaps():
            copy.wait()
        total = g_feat[0]
        for i in range(1, 8):
            total = total + g_feat[i]
        g[gram_rows(q), :] = total
        for copy in gram_gathers():
            copy.start()

    def eliminate(first, last):
        small_row = lax.broadcasted_iota(jnp.int32, (16, K), 0)
        wide_row = lax.broadcasted_iota(jnp.int32, (K, 2 * K), 0)

        def panel(i, _):
            at = pl.ds(pl.multiple_of(i * 16, 16), 16)
            left, right = work[at, :K], work[at, K:]
            block = pltpu.roll(left, (K - i * 16) % K, 1)
            column = [jnp.broadcast_to(block[:, j : j + 1], (16, K)) for j in range(16)]
            pivots = jnp.ones((16, K), F32)
            for j in range(16):
                pivot = jnp.broadcast_to(column[j][j : j + 1, :], (16, K))
                ratio = jnp.where(small_row > j, column[j] * (1.0 / pivot), 0.0)
                pivots = jnp.where(small_row == j, pivot, pivots)
                for k in range(j + 1, 16):
                    column[k] = column[k] - ratio * column[k][j : j + 1, :]
                left = left - ratio * left[j : j + 1, :]
                right = right - ratio * right[j : j + 1, :]
            scale = lax.rsqrt(pivots)
            scale = scale * (1.5 - 0.5 * pivots * scale * scale)
            fresh = jnp.concatenate([left * scale, right * scale], axis=1)
            update = full(fresh[:, :K], fresh, (0, 0))
            work[...] = jnp.where(wide_row >= i * 16 + 16, work[...] - update, work[...])
            work[at, :] = fresh
            return 0

        lax.fori_loop(first, last, panel, 0)

    def factor_start():
        for copy in gram_gathers():
            copy.wait()
        work[:, :K] = g[...]
        work[:, K:] = (lane == row).astype(F32)
        eliminate(0, FIRST)

    def factor_middle():
        eliminate(FIRST, SECOND)

    def factor_end():
        eliminate(SECOND, 8)
        inverse[...] = work[:, K:]

    def p_copy(r, h):
        mine = half_rows(feat, h)
        return to_feat(r, p.at[mine, :], p.at[mine, :], p_ssem.at[h], p_rsem.at[h])

    def v_copy(r, h):
        rows = part_rows(q_peer(r), h)
        return to_dp(r, v_send.at[rows, :], v_recv.at[r, h], v_ssem.at[h], v_rsem.at[h])

    def w_copy(r, h):
        mine = part_rows(q, h)
        return to_dp(r, v.at[mine, :], v.at[mine, :], w_ssem.at[h], w_rsem.at[h])

    def part_rows(i, h):
        return pl.ds(pl.multiple_of(i * 128 + h * 64, 64), 64)

    def c_copy(r):
        return to_dp(r, c_recv.at[q], c_recv.at[q], c_ssem, c_rsem)

    def count_documents():
        ids_copy.wait()
        counts = jnp.zeros((1, K), F32)
        for i in range(16):
            column = jnp.broadcast_to(ids[i : i + 1, :].astype(F32), (K, K)).T
            counts = counts + jnp.sum((column == lane.astype(F32)).astype(F32), axis=0, keepdims=True)
        c_recv[q] = jnp.broadcast_to(counts, (8, K))
        for r in range(7):
            c_copy(r).start()

    def receive_rest():
        for i in range(4):
            x_copies[i].wait()
            x[1024 + i * 256 : 1280 + i * 256, :] = x_recv[i * 256 : (i + 1) * 256, :].astype(BF16)

    def transpose(h):
        for c in range(4 * h, 4 * h + 4):
            xt[c] = x[c * 256 : (c + 1) * 256, :].T

    def sweep(step, _):
        split[...] = pieces(v[...])
        pl.when(step > 0)(gram_swap)

        @pl.when((step == 0) & (core == 1))
        def _():
            pl.semaphore_wait(late_sem, 1)

        project_half(0, True)

        @pl.when(step == 0)
        def _():
            transpose(0)
            receive_rest()

        project_half(1, True)
        pl.when(step > 0)(gram_gather)

        p[half_rows(feat, 0), :] = projected(0)
        for r in range(7):
            p_copy(r, 0).start()
        p[half_rows(feat, 1), :] = projected(1)
        for r in range(7):
            p_copy(r, 1).start()

        pl.when(step > 0)(factor_start)

        @pl.when(step == 0)
        def _():
            transpose(1)
            count_documents()

        for h in range(2):
            for dz in (0, 1, 3, 2):
                for r in range(7):
                    if OFFSETS[r][0] == dz:
                        p_copy(r, h).wait()
                j = (fz + 4 - dz) % 4
                part = joined(times(xt[h * 4 + j], pieces(p[pair_rows(j, h), :])))
                if h == 0 and dz == 0:
                    v_send[...] = part
                else:
                    v_send[...] += part
            if h == 0:
                pl.when(step > 0)(factor_middle)

        @pl.when((step == 0) & (core == 0))
        def _():
            pl.semaphore_signal(late_sem, inc=1, device_id={"dp": q * 2 + 1}, device_id_type=MESH)

        for h in range(2):
            for r in range(7):
                v_copy(r, h).start()

        pl.when(step > 0)(factor_end)

        for h in range(2):
            for r in range(7):
                v_copy(r, h).wait()
            total = v_send[part_rows(q, h), :]
            for r in range(7):
                total = total + v_recv[r, h]
            v[part_rows(q, h), :] = full(total, inverse[...], (1, 1))
            for r in range(7):
                w_copy(r, h).start()
        gram_scatter()
        for h in range(2):
            for r in range(7):
                w_copy(r, h).wait()
        return 0

    lax.fori_loop(0, ITERS, sweep, 0)

    split[...] = pieces(v[...])
    gram_swap()
    project_half(0, True)
    project_half(1, False)
    gram_gather()
    for r in range(7):
        y_copy(r, 1).start()
    for r in range(7):
        c_copy(r).wait()
    counts = c_recv[0]
    for i in range(1, 8):
        counts = counts + c_recv[i]
    counts = counts[0:1, :]
    documents = 2 * lax.axis_size("dp")
    share = jnp.where(counts > 0, 1.0 / (documents * jnp.maximum(counts, 1.0)), 0.0)
    weight = []
    for i in range(2):
        column = jnp.broadcast_to(ids[pl.ds(i * 8 + feat, 1), :].astype(F32), (K, K)).T
        weight.append(
            jnp.sum(jnp.where(column == lane.astype(F32), share, 0.0), axis=1, keepdims=True)
        )
    factor_start()
    factor_middle()
    factor_end()
    total = jnp.concatenate([projected(0), projected(1)], axis=0)
    proj_mine[...] = full(total, inverse[...], (1, 1))
    proj_copies = [
        to_core(i, proj_mine.at[mine, :], proj_other.at[theirs, :])
        for i, mine, theirs in ((1, slice(0, 128), slice(128, 256)), (4, slice(128, 256), slice(0, 128)))
    ]
    for copy in proj_copies:
        copy.start()
    for copy in proj_copies:
        copy.wait()
    proj_act = jnp.where(even, proj_mine[...], proj_other[...])
    proj_grad = jnp.where(even, proj_other[...], proj_mine[...])
    left = jnp.concatenate(weight, axis=0) * proj_grad * proj_grad
    s_part[...] = full(left, proj_act * proj_act, (0, 0))

    half = pl.ds(pl.multiple_of(core * 64, 64), 64)
    s_feat[feat] = s_part[half, :]
    copies = [to_feat(r, s_feat.at[feat], s_feat.at[feat], sf_ssem, sf_rsem) for r in range(7)]
    for copy in copies:
        copy.start()
    basis_mine[...] = full(v[...], inverse[...], (1, 1))
    basis_copy = to_core(2, basis_mine, basis_other)
    basis_copy.start()
    for copy in copies:
        copy.wait()
    total = s_feat[0]
    for i in range(1, 8):
        total = total + s_feat[i]
    s_dp[q] = total
    copies = [to_dp(r, s_dp.at[q], s_dp.at[q], sd_ssem, sd_rsem) for r in range(7)]
    for copy in copies:
        copy.start()
    basis_copy.wait()
    basis_act_ref[...] = jnp.where(even, basis_mine[...], basis_other[...])
    basis_grad_ref[...] = jnp.where(even, basis_other[...], basis_mine[...])
    for copy in copies:
        copy.wait()
    total = s_dp[0]
    for i in range(1, 8):
        total = total + s_dp[i]
    s_mine[...] = total
    s_copy = to_core(3, s_mine, s_other)
    s_copy.start()
    s_copy.wait()
    scales_ref[half, :] = s_mine[...]
    scales_ref[pl.ds(pl.multiple_of((1 - core) * 64, 64), 64), :] = s_other[...]


def local(activations, gradients, start_act, start_grad, doc_ids):
    vmem = pl.BlockSpec(memory_space=pltpu.VMEM)
    hbm = pl.BlockSpec(memory_space=pl.ANY)
    dma = pltpu.SemaphoreType.DMA
    return pl.pallas_call(
        kernel,
        out_shape=(
            jax.ShapeDtypeStruct((1024, K), F32),
            jax.ShapeDtypeStruct((1024, K), F32),
            jax.ShapeDtypeStruct((K, K), F32),
        ),
        in_specs=[hbm] * 5,
        out_specs=(vmem,) * 3,
        scratch_shapes=[
            pltpu.VMEM((1024, 1024), BF16),
            pltpu.VMEM((1024, 1024), F32),
            pltpu.VMEM((1024, 1024), F32),
            pltpu.VMEM((2048, 1024), BF16),
            pltpu.VMEM((8, 1024, 256), BF16),
            pltpu.VMEM((1024, 2 * K), BF16),
            pltpu.VMEM((2048, K), F32),
            pltpu.VMEM((7, 2, 128, K), F32),
            pltpu.VMEM((2048, K), F32),
            pltpu.VMEM((1024, K), F32),
            pltpu.VMEM((7, 2, 64, K), F32),
            pltpu.VMEM((1024, K), F32),
            pltpu.VMEM((K, K), F32),
            pltpu.VMEM((7, 16, K), F32),
            pltpu.VMEM((8, 16, K), F32),
            pltpu.VMEM((K, K), F32),
            pltpu.VMEM((K, 2 * K), F32),
            pltpu.VMEM((K, K), F32),
            pltpu.VMEM((16, K), jnp.int32),
            pltpu.VMEM((8, 8, K), F32),
            pltpu.VMEM((256, K), F32),
            pltpu.VMEM((256, K), F32),
            pltpu.VMEM((1024, K), F32),
            pltpu.VMEM((1024, K), F32),
            pltpu.VMEM((K, K), F32),
            pltpu.VMEM((8, 64, K), F32),
            pltpu.VMEM((8, 64, K), F32),
            pltpu.VMEM((64, K), F32),
            pltpu.VMEM((64, K), F32),
            dma((7,)), dma((2, 4)),
            dma((2, 7)), dma((2, 7)), dma((2, 7)), dma((2, 7)),
            dma((2, 7)), dma((2, 7)), dma((2, 7)), dma((2, 7)),
            dma((7,)), dma((7,)), dma((7,)), dma((7,)), dma((7,)), dma((7,)), dma((7,)), dma((7,)),
            dma((5,)), dma((5,)),
            dma((7,)), dma((7,)), dma((7,)), dma((7,)), pltpu.SemaphoreType.REGULAR,
        ],
        compiler_params=pltpu.CompilerParams(
            collective_id=0, has_side_effects=True, vmem_limit_bytes=50 * 2**20
        ),
        name="subspace",
    )(activations, gradients, start_act, start_grad, doc_ids.reshape(8, 128))


def solution(mesh):
    placed = (P("dp", "feat"), P("dp", "feat"), P("feat", None), P("feat", None), P("dp"))
    return jax.shard_map(
        local,
        mesh=mesh,
        in_specs=placed,
        out_specs=(P("feat", None), P("feat", None), P()),
        check_vma=False,
    )
```
